32 devices in a mesh: dp: 2 (over x), expert: 16 (over z, y, core).
Axes of the slice: x: 2, y: 2, z: 4, core: 2. Of those that a mesh axis runs over, the one named last changes fastest.
Arguments:
- tokens_in: bfloat16 [4096, 3584], P(('dp', 'expert')), may hold values from -6 to 6
- out_grad: bfloat16 [4096, 3584], P(('dp', 'expert')), may hold values from -0.59765625 to 0.59765625
- router_logits: float32 [4096, 192], P(('dp', 'expert')), may hold values from -12 to 250
- expert_ids: int32 [4096, 8], P(('dp', 'expert')), may hold values from 0 to 191, all different within a row; in each aligned block of 128 rows (0 to 127, 128 to 255, ...) at most 8 rows name the same one
- saved_hidden: bfloat16 [2, 16, 16, 8, 1024], P('dp', 'expert'), may hold values from -6 to 6
- down_weight: bfloat16 [16, 1024, 3584], P('expert', 'dp'), may hold values from -0.1875 to 0.1875
Outputs:
- hidden_grad: bfloat16 [2, 16, 16, 8, 1024], P('dp', 'expert')
- logit_grad: float32 [4096, 192], P(('dp', 'expert'))
- router_grad: float32 [3584, 192], P('expert', 'dp')
The draws below stay inside these ranges and needn't reach their ends.
Inputs may be any that keep to these rules, and one draw needn't show every extreme that they name: `expert_ids`: among the 128 rows of one device no expert is named by more than 8 rows, a bound that some block reaches.
All inputs are finite; a program needn't handle non-finite values.
Results may differ from the reference program's by a relative error of at most 0.013.
Values may be sent and summed in bfloat16 or wider, within the bound.
No kernel may reach another device: no remote copies, remote signals or barrier semaphores. Data moves between devices by JAX's collectives and lax.ppermute only.
A program may use at most 64 MiB of HBM per device.

```python
import math
import jax
import jax.numpy as jnp
import numpy as np
from jax import lax

D = 3584
FW = 1024
EXPERTS = 192
TOPK = 8
TOK_DEV = 128
CAP = 8
TOKENS = 4096
N_DP = 2
N_EXPERT = 16


def draw_router_logits(key, part):
    first_key = jax.random.fold_in(key, 0)
    base = jnp.clip(2.0 * jax.random.normal(first_key, (TOKENS, EXPERTS), jnp.float32), -12.0, 12.0)
    return base


def steps_of(own_key, dims, pieces, least, top_value):
    level = 1.0
    for position, blocks in pieces:
        draws = jax.random.uniform(jax.random.fold_in(jax.random.fold_in(own_key, 6), position), (blocks,), jnp.float32, least / len(pieces), top_value / len(pieces))
        level = level * jnp.repeat(jnp.exp(draws), dims[position] // blocks).reshape((-1,) + (1,) * (len(dims) - 1 - position))
    return level


def routed_block(own_key, own, number, rows, count, top, reach, slope):
    order = jax.random.permutation(own_key, count)
    heavy_load, common = portions_of(count, rows * top, reach, slope, True), portions_of(count, rows * top, reach, slope, False)
    places = jnp.arange(count)

    def named(lengths, rotation):
        used = int((lengths > 0).sum())
        fixed = max(1, used // 4)
        moved = fixed + (places - fixed + rotation * (used - fixed)) % max(1, count - fixed)
        return jnp.zeros((count,), jnp.int32).at[order[jnp.where(places < fixed, places, moved)]].set(jnp.asarray(lengths, jnp.int32))

    lengths = jnp.where(number % 4 == 0, named(heavy_load, number // 4), named(common, number - number // 4 - 1))
    mixed = jax.random.permutation(jax.random.fold_in(own, 3), count)
    giver, sink = mixed[0:count // 2 * 2:2], mixed[1:count // 2 * 2:2]
    slack = jnp.minimum(lengths[giver] - 1, reach - lengths[sink]) // 2
    slack = jnp.where((giver == order[0]) | (sink == order[0]) | (lengths[sink] == 0), 0, jnp.maximum(slack, 0))
    moved = jax.random.randint(jax.random.fold_in(own, 4), (count // 2,), 0, 1 << 20) % (slack + 1)
    lengths = lengths.at[giver].add(-moved).at[sink].add(moved)
    labels = jnp.searchsorted(jnp.cumsum(lengths), jnp.arange(rows * top), side="right").astype(jnp.int32)
    grid = labels.reshape(top, rows).T
    grid = grid[jax.random.permutation(jax.random.fold_in(own, 1), rows)]
    rotation = jax.random.randint(jax.random.fold_in(own, 2), (rows, 1), 0, top)
    return jnp.take_along_axis(grid, (jnp.arange(top)[None, :] + rotation) % top, axis=1)


def portions_of(amount, total, reach, skew, full):
    weights = [(1 << 20) // math.isqrt(grade ** skew) + 1 for grade in range(1, amount + 1)]
    largest = reach if full else min(reach, max(-(-total // amount), total * weights[0] // sum(weights)))
    least = 1 if total - largest >= amount - 1 else 0
    given, surplus = [largest] + [least] * (amount - 1), total - largest - least * (amount - 1)
    while surplus > 0:
        free = [i for i in range(1, amount) if given[i] < largest] or [i for i in range(1, amount) if given[i] < reach]
        pool, budget = sum([weights[i] for i in free]), surplus
        for i in free:
            addition = min(reach - given[i], max(1, budget * weights[i] // pool), surplus)
            given[i] = given[i] + addition
            surplus = surplus - addition
    return np.array(given)


def centred(key, shape, deviation, reach, cuts=(), held_as=jnp.bfloat16):
    result = jax.random.normal(key, shape, jnp.float32) * deviation
    if len(cuts) > 0:
        result = steps_of(key, shape, cuts, -0.22, 0.18) * result
    return jnp.clip(result, min=-reach, max=reach).astype(held_as)


def setup_inputs(seed: int = 0) -> dict:
    key_list = jax.random.split(jax.random.key(seed), 7)
    tokens_in = centred(key_list[0], (TOKENS, D), 1.0, 6.0, ((0, 32),))
    out_grad = centred(key_list[1], (TOKENS, D), 0.1, 0.59765625, ((0, 32),))
    router_logits = draw_router_logits(jax.random.fold_in(key_list[6], 71), 0)
    expert_ids_keys = jax.random.split(jax.random.fold_in(key_list[3], 1), TOKENS // TOK_DEV)
    expert_ids_turns = jax.random.permutation(jax.random.fold_in(key_list[3], 3), TOKENS // TOK_DEV)
    expert_ids = jax.vmap(lambda own, number: routed_block(jax.random.fold_in(key_list[3], 2), own, number, TOK_DEV, EXPERTS, TOPK, CAP, 2))(expert_ids_keys, expert_ids_turns).reshape((TOKENS, TOPK))
    saved_hidden = centred(key_list[4], (N_DP, N_EXPERT, N_EXPERT, CAP, FW), 1.0, 6.0, ((0, 2), (1, 16)))
    down_weight = centred(key_list[5], (N_EXPERT, FW, D), FW ** -0.5, 0.1875, ((0, 16), (1, 2)))
    return dict(tokens_in=tokens_in, out_grad=out_grad, router_logits=router_logits, expert_ids=expert_ids, saved_hidden=saved_hidden, down_weight=down_weight)


RSCALE = 2.827
ZLOSS = 0.25


def slot_table(ids_block, flight, cap):
    owners = jnp.arange(flight, dtype=jnp.int32)
    chosen = jnp.any(ids_block[:, :, None] == owners[None, None, :], axis=1)
    as_int = chosen.astype(jnp.int32)
    rank = jnp.cumsum(as_int, axis=0) - as_int
    places = jnp.arange(cap, dtype=jnp.int32)
    table = chosen[None, :, :] & (rank[None, :, :] == places[:, None, None])
    return jnp.transpose(table, (2, 0, 1))


def gate_parts(logits, ids):
    top = jnp.max(logits, axis=1, keepdims=True)
    shifted = jnp.exp(logits - top)
    total = jnp.sum(shifted, axis=1, keepdims=True)
    probs = shifted / total
    lse = top + jnp.log(total)
    columns = jnp.arange(logits.shape[1], dtype=jnp.int32)
    picks = (ids[:, :, None] == columns[None, None, :]).astype(jnp.float32)
    chosen_logit = jnp.sum(picks * logits[:, None, :], axis=2)
    scores = jax.nn.sigmoid(chosen_logit)
    ssum = jnp.sum(scores, axis=1, keepdims=True)
    gates = RSCALE * scores / ssum
    return probs, lse, picks, scores, ssum, gates


def reference(tokens_in, out_grad, router_logits, expert_ids, saved_hidden, down_weight):
    rows = TOK_DEV * N_EXPERT
    highest = lax.Precision.HIGHEST

    def group(index):
        start = index * rows
        xin = lax.dynamic_slice_in_dim(tokens_in, start, rows, 0)
        dyin = lax.dynamic_slice_in_dim(out_grad, start, rows, 0)
        logits = lax.dynamic_slice_in_dim(router_logits, start, rows, 0)
        ids = lax.dynamic_slice_in_dim(expert_ids, start, rows, 0)
        probs, lse, picks, scores, ssum, gates = gate_parts(logits, ids)
        gate_half = gates.astype(jnp.bfloat16)
        in_window = picks[:, :, :N_EXPERT]
        gate_te = jnp.sum(in_window * gate_half.astype(jnp.float32)[:, :, None], axis=1)
        gate_blocks = gate_te.reshape(N_EXPERT, TOK_DEV, N_EXPERT)
        tables = jax.vmap(lambda blk: slot_table(blk, N_EXPERT, CAP))(ids.reshape(N_EXPERT, TOK_DEV, TOPK))
        dy_blocks = dyin.astype(jnp.float32).reshape(N_EXPERT, TOK_DEV, D)
        hidden_here = saved_hidden[index]

        def owner(expert):
            tab = tables[:, expert].astype(jnp.float32)
            recv = jnp.einsum('sct,std->scd', tab, dy_blocks, precision=highest).astype(jnp.bfloat16)
            weight = down_weight[expert]
            grads = jnp.dot(recv.reshape(N_EXPERT * CAP, D), weight.T, preferred_element_type=jnp.float32)
            gslot = jnp.einsum('sct,st->sc', tab, gate_blocks[:, :, expert], precision=highest)
            dhid = (gslot.reshape(-1, 1) * grads).astype(jnp.bfloat16).reshape(N_EXPERT, CAP, FW)
            saved = hidden_here[expert].reshape(N_EXPERT * CAP, FW).astype(jnp.float32)
            dgate = jnp.sum(saved * grads, axis=1).reshape(N_EXPERT, CAP)
            back = jnp.einsum('sct,sc->st', tab, dgate, precision=highest)
            return dhid, back

        dhid_all, back_all = lax.map(owner, jnp.arange(N_EXPERT, dtype=jnp.int32))
        grad_te = jnp.transpose(back_all, (1, 2, 0)).reshape(rows, N_EXPERT)
        grad_choice = jnp.sum(in_window * grad_te[:, None, :], axis=2)
        mixed = jnp.sum(grad_choice * gates, axis=1, keepdims=True) / RSCALE
        dscore = (RSCALE / ssum) * (grad_choice - mixed)
        dchosen = dscore * scores * (1.0 - scores)
        lgrad = jnp.sum(picks * dchosen[:, :, None], axis=1) + 2.0 * ZLOSS * lse * probs
        panel = jnp.dot(xin.astype(jnp.float32).T, lgrad, precision=highest)
        return dhid_all, lgrad, panel

    dhid, lgrad, panels = lax.map(group, jnp.arange(N_DP, dtype=jnp.int32))
    return dhid, lgrad.reshape(TOKENS, EXPERTS), jnp.sum(panels, axis=0)
```

```python
import jax
import jax.numpy as jnp
from jax import lax
from jax.experimental import pallas as pl
from jax.experimental.pallas import tpu as pltpu
from jax.sharding import PartitionSpec as P

RSCALE = 2.827
ZLOSS = 0.25


def entering(shard, axis, combine, identity):
    length, place = (lax.axis_size(axis), lax.axis_index(axis))
    everything = lax.all_gather(shard.astype(jnp.bfloat16), axis)
    start = jnp.broadcast_to(jnp.asarray(identity, shard.dtype), shard.shape)

    def lap(k, before):
        reached = k < place
        new = combine(before, everything[k].astype(shard.dtype))
        return jnp.where(reached, new, before)

    return lax.fori_loop(0, length, lap, start)


def from_root(value, axis, source):
    kept = jnp.where(lax.axis_index(axis) == source, value, 0).astype(value.dtype)
    return lax.psum(kept, axis)


def slot_table(ids_block, flight, cap):
    owners = jnp.arange(flight, dtype=jnp.int32)
    chosen = jnp.any(ids_block[:, :, None] == owners[None, None, :], axis=1)
    as_int = chosen.astype(jnp.int32)
    rank = jnp.cumsum(as_int, axis=0) - as_int
    places = jnp.arange(cap, dtype=jnp.int32)
    table = chosen[None, :, :] & (rank[None, :, :] == places[:, None, None])
    return jnp.transpose(table, (2, 0, 1))


def own_columns(panel):
    count = panel.shape[1] // lax.axis_size("dp")
    return lax.dynamic_slice_in_dim(panel, lax.axis_index("dp") * count, count, 1)


def general_local(tokens_in, out_grad, router_logits, expert_ids, saved_hidden, down_weight):
    highest = lax.Precision.HIGHEST
    flight = lax.axis_size("expert")
    cap = saved_hidden.shape[3]
    hidden = saved_hidden.shape[4]
    width = out_grad.shape[1]
    experts = router_logits.shape[1]
    top = jnp.max(router_logits, axis=1, keepdims=True)
    shifted = jnp.exp(router_logits - top)
    total = jnp.sum(shifted, axis=1, keepdims=True)
    probs = shifted / total
    lse = top + jnp.log(total)
    columns = jnp.arange(experts, dtype=jnp.int32)
    picks = (expert_ids[:, :, None] == columns[None, None, :]).astype(jnp.float32)
    chosen_logit = jnp.sum(picks * router_logits[:, None, :], axis=2)
    scores = jax.nn.sigmoid(chosen_logit)
    ssum = jnp.sum(scores, axis=1, keepdims=True)
    gates = RSCALE * scores / ssum
    gate_half = gates.astype(jnp.bfloat16)
    in_window = picks[:, :, :flight]
    gate_te = jnp.sum(in_window * gate_half.astype(jnp.float32)[:, :, None], axis=1)
    table = slot_table(expert_ids, flight, cap)
    table_half = table.astype(jnp.bfloat16)
    table_full = table.astype(jnp.float32)
    send_rows = jnp.einsum(
        "ect,td->ecd", table_half, out_grad, preferred_element_type=jnp.float32
    ).astype(jnp.bfloat16)
    send_gates = jnp.einsum("ect,te->ec", table_full, gate_te, precision=highest).astype(
        jnp.bfloat16
    )
    recv_rows, recv_gates = (
        lax.all_to_all(send_rows, "expert", split_axis=0, concat_axis=0, tiled=True),
        lax.all_to_all(send_gates, "expert", split_axis=0, concat_axis=0, tiled=True),
    )
    flat_rows = recv_rows.reshape(flight * cap, width)
    part = lax.dot_general(
        flat_rows,
        lax.all_gather(down_weight, "dp", axis=1, tiled=True)[0],
        (((1,), (1,)), ((), ())),
        preferred_element_type=jnp.float32,
    )
    slot_gates = recv_gates.reshape(flight * cap, 1).astype(jnp.float32)
    hidden_grad = (slot_gates * part).astype(jnp.bfloat16).reshape(1, 1, flight, cap, hidden)
    saved_flat = saved_hidden.reshape(flight * cap, hidden)
    gate_grad = jnp.sum(saved_flat * part, axis=1).reshape(flight, cap)
    returned = lax.all_to_all(gate_grad, "expert", split_axis=0, concat_axis=0, tiled=True)
    grad_te = jnp.einsum("ect,ec->te", table_full, returned, precision=highest)
    grad_choice = jnp.sum(in_window * grad_te[:, None, :], axis=2)
    mixed = jnp.sum(grad_choice * gates, axis=1, keepdims=True) / RSCALE
    dscore = RSCALE / ssum * (grad_choice - mixed)
    dchosen = dscore * scores * (1.0 - scores)
    logit_grad = jnp.sum(picks * dchosen[:, :, None], axis=1) + 2.0 * ZLOSS * lse * probs
    tokens_full = tokens_in.astype(jnp.float32)
    own_rows = lax.psum_scatter(
        lax.dot_general(tokens_full, logit_grad, (((0,), (0,)), ((), ())), precision=highest),
        "expert",
        scatter_dimension=0,
        tiled=True,
    )
    before = entering(
        own_rows, "dp", lambda earlier, later: earlier + later, jnp.zeros_like(own_rows)
    )
    finished = before + own_rows
    spread = from_root(finished.astype(jnp.bfloat16), "dp", lax.axis_size("dp") - 1).astype(
        finished.dtype
    )
    router_grad = own_columns(spread)
    return (hidden_grad, logit_grad, router_grad)


NT = (((1,), (1,)), ((), ()))
NN = (((1,), (0,)), ((), ()))
VMEM_LIMIT = 48 * 1024 * 1024


def kernel_call(body, out_shape, name, flops, touched, *operands, smem=0):
    specs = [
        pl.BlockSpec(memory_space=pltpu.SMEM if k < smem else pltpu.VMEM)
        for k in range(len(operands))
    ]
    return pl.pallas_call(
        body,
        out_shape=out_shape,
        in_specs=specs,
        out_specs=jax.tree.map(lambda _: pl.BlockSpec(memory_space=pltpu.VMEM), out_shape),
        compiler_params=pltpu.CompilerParams(vmem_limit_bytes=VMEM_LIMIT),
        cost_estimate=pl.CostEstimate(flops=flops, bytes_accessed=touched, transcendentals=0),
        name=name,
    )(*operands)


def iota(shape, dim):
    return lax.broadcasted_iota(jnp.int32, shape, dim)


def three_halves(value):
    high = value.astype(jnp.bfloat16)
    rest = value - high.astype(jnp.float32)
    middle = rest.astype(jnp.bfloat16)
    low = (rest - middle.astype(jnp.float32)).astype(jnp.bfloat16)
    return high, middle, low


def ranks(chosen):
    tokens = chosen.shape[1]
    before = (iota((tokens, tokens), 0) < iota((tokens, tokens), 1)).astype(jnp.bfloat16)
    return lax.dot_general(
        chosen.astype(jnp.bfloat16), before, NN, preferred_element_type=jnp.float32
    )


def route_body(logits_ref, ids_ref, z_ref, a_ref, bundle_ref, *, flight):
    logits = logits_ref[...]
    ids = ids_ref[...]
    experts, tokens = logits.shape
    topk = ids.shape[0]
    top = jnp.max(logits, axis=0, keepdims=True)
    shifted = jnp.exp(logits - top)
    total = jnp.sum(shifted, axis=0, keepdims=True)
    lse = top + jnp.log(total)
    z = (2.0 * ZLOSS) * lse * (shifted / total)
    z_ref[...] = z
    rows = iota((experts, tokens), 0)
    chosen = [
        jnp.sum(jnp.where(rows == ids[k : k + 1], logits, 0.0), axis=0, keepdims=True)
        for k in range(topk)
    ]
    scores = jax.nn.sigmoid(jnp.concatenate(chosen, axis=0))
    ssum = jnp.sum(scores, axis=0, keepdims=True)
    gates = RSCALE * scores / ssum
    slope = (RSCALE / ssum) * scores * (1.0 - scores)
    dense = jnp.zeros((experts, tokens), jnp.float32)
    window = iota((flight, tokens), 0)
    gate_te = jnp.zeros((flight, tokens), jnp.float32)
    picked = jnp.zeros((flight, tokens), jnp.float32)
    for k in range(topk):
        dense = jnp.where(rows == ids[k : k + 1], slope[k : k + 1], dense)
        gate_te = jnp.where(window == ids[k : k + 1], gates[k : k + 1], gate_te)
        picked = jnp.where(window == ids[k : k + 1], 1.0, picked)
    a_ref[...] = dense
    slot = jnp.where(picked > 0.0, ranks(picked), -1.0)
    high, middle, low = three_halves(gate_te)
    bundle_ref[0:experts] = z.astype(jnp.bfloat16)
    bundle_ref[experts : experts + 16] = jnp.concatenate(
        [ids.astype(jnp.float32), slope], axis=0
    ).astype(jnp.bfloat16)
    bundle_ref[experts + 16 : experts + 32] = slot.astype(jnp.bfloat16)
    bundle_ref[experts + 32 : experts + 48] = high
    bundle_ref[experts + 48 : experts + 64] = middle
    bundle_ref[experts + 64 : experts + 80] = low


def pack_body(place_ref, ids_ref, ids_peer_ref, out_grad_ref, out_grad_peer_ref, *outs, cap):
    me = place_ref[1]
    parts = []
    for ids_one, grad_one in ((ids_ref, out_grad_ref), (ids_peer_ref, out_grad_peer_ref)):
        ids = ids_one[...]
        topk, tokens = ids.shape
        wanted = (iota((8, tokens), 0) * 2) ^ me
        picked = jnp.zeros((8, tokens), jnp.float32)
        for k in range(topk):
            picked = jnp.where(wanted == ids[k : k + 1], 1.0, picked)
        slot = jnp.where(picked > 0.0, ranks(picked), -1.0)
        place = iota((cap, tokens), 0).astype(jnp.float32)
        select = jnp.concatenate(
            [jnp.where(slot[q : q + 1] == place, 1.0, 0.0) for q in range(8)], axis=0
        )
        parts.append(
            lax.dot_general(
                select.astype(jnp.bfloat16), grad_one[...], NN, preferred_element_type=jnp.float32
            )
        )
    for q, out in enumerate(outs):
        rows = slice(q * cap, (q + 1) * cap)
        out[...] = jnp.concatenate([parts[0][rows], parts[1][rows]], axis=0).astype(jnp.bfloat16)


def turn_body(tokens_ref, out_ref):
    out_ref[...] = tokens_ref[...].T


def swap_matrix(me, size, cap, dtype):
    return (iota((size, size), 1) == (iota((size, size), 0) ^ (me * cap))).astype(dtype)


def grads_body(place_ref, saved_ref, saved_other_ref, weight_ref, *refs, cap):
    pieces, (own_ref, other_ref, gate_ref) = refs[:16], refs[16:]
    dp, me = place_ref[0], place_ref[1]
    weight = weight_ref[...]
    slots = saved_ref.shape[0]
    swap = swap_matrix(me, slots, cap, jnp.bfloat16)
    where_to = swap_matrix(me, slots, cap, jnp.float32)
    lines = []
    for half, saved_one in enumerate((saved_ref, saved_other_ref)):
        rows = jnp.concatenate([p[...] for p in pieces[half * 8 : half * 8 + 8]], axis=0)
        grads = lax.dot_general(rows, weight, NT, preferred_element_type=jnp.float32)
        saved = lax.dot_general(swap, saved_one[...], NN, preferred_element_type=jnp.float32)
        if half == 0:
            own_ref[...] = grads
        else:
            other_ref[...] = grads.astype(jnp.bfloat16)
        sums = jnp.sum(saved * grads, axis=1, keepdims=True)
        lines.append(jnp.sum(where_to * sums, axis=0, keepdims=True))
    count = gate_ref.shape[0] // 2
    for k in range(2):
        line = jnp.where(dp == k, lines[0], lines[1])
        gate_ref[k * count : (k + 1) * count] = jnp.broadcast_to(
            line[None], (count, 1, line.shape[1])
        )


def hidden_body(place_ref, own_ref, other_ref, *refs, cap, experts):
    bundles, out_ref = refs[:4], refs[4]
    dp, me = place_ref[0], place_ref[1]
    slots, half = own_ref.shape
    tokens = bundles[0].shape[2]
    mine = iota((16, tokens), 0) == me
    place = iota((cap, tokens), 0).astype(jnp.float32)
    columns = []
    for r in range(16):
        bundle = bundles[r % 4]
        slot = bundle[r // 4, experts + 16 : experts + 32].astype(jnp.float32)
        gate = bundle[r // 4, experts + 32 : experts + 48].astype(jnp.float32)
        slot = jnp.sum(jnp.where(mine, slot, 0.0), axis=0, keepdims=True)
        gate = jnp.sum(jnp.where(mine, gate, 0.0), axis=0, keepdims=True)
        columns.append(jnp.sum(jnp.where(slot == place, gate, 0.0), axis=1, keepdims=True))
    gates = jnp.concatenate(columns, axis=0)
    swap = swap_matrix(me, slots, cap, jnp.bfloat16)
    for k, part in enumerate((own_ref, other_ref)):
        value = (gates * part[...].astype(jnp.float32)).astype(jnp.bfloat16)
        value = lax.dot_general(swap, value, NN, preferred_element_type=jnp.float32)
        start = pl.multiple_of((dp if k == 0 else 1 - dp) * half, 128)
        out_ref[:, pl.ds(start, half)] = value.astype(jnp.bfloat16)


def panel_body(place_ref, z_ref, a_ref, gate_ref, turned_ref, *refs, cap, experts):
    bundles, (logit_ref, keep_ref, send_ref) = refs[:4], refs[4:7]
    dp, me = place_ref[0], place_ref[1]
    tokens = z_ref.shape[1]
    both = jnp.concatenate([gate_ref[k] for k in range(gate_ref.shape[0])], axis=0)
    gate_abs = both[:16] + both[16:]
    swap = swap_matrix(me, gate_abs.shape[1], cap, jnp.bfloat16)
    gate_rel = sum(
        lax.dot_general(part, swap, NN, preferred_element_type=jnp.float32)
        for part in three_halves(gate_abs)
    )
    rows = iota((experts, tokens), 0).astype(jnp.float32)
    lines, blocks = [], []
    total = None
    for r in range(16):
        bundle = bundles[r % 4]
        slot = bundle[r // 4, experts + 16 : experts + 32].astype(jnp.float32)
        gate = sum(
            bundle[r // 4, experts + 32 + 16 * k : experts + 48 + 16 * k].astype(jnp.float32)
            for k in (2, 1, 0)
        )
        grad = jnp.zeros((16, tokens), jnp.float32)
        for c in range(cap):
            grad = jnp.where(slot == float(c), gate_rel[:, r * cap + c : r * cap + c + 1], grad)
        mixed = jnp.sum(grad * gate, axis=0, keepdims=True) / RSCALE
        spread = jnp.concatenate(
            [grad - mixed, jnp.broadcast_to(-mixed, (experts - 16, tokens))], axis=0
        )
        if r == 0:
            line = z_ref[...] + a_ref[...] * spread
            logit_ref[...] = line
        else:
            pairs = bundle[r // 4, experts : experts + 16].astype(jnp.float32)
            dense = jnp.zeros((experts, tokens), jnp.float32)
            for k in range(8):
                dense = jnp.where(rows == pairs[k : k + 1], pairs[8 + k : 9 + k], dense)
            line = bundle[r // 4, 0:experts].astype(jnp.float32) + dense * spread
        lines.append(line.astype(jnp.bfloat16))
        blocks.append(turned_ref[me ^ r])
        if len(lines) == 2:
            part = lax.dot_general(
                jnp.concatenate(lines, axis=1),
                jnp.concatenate(blocks, axis=1),
                NT,
                preferred_element_type=jnp.float32,
            )
            total = part if total is None else total + part
            lines, blocks = [], []
    count = keep_ref.shape[0]
    first, second = total[:count], total[count:]
    keep_ref[...] = jnp.where(dp == 0, first, second)
    send_ref[...] = jnp.where(dp == 0, second, first).astype(jnp.bfloat16)


def over_dp(value):
    return lax.ppermute(value, "dp", [(0, 1), (1, 0)])


def over_expert(value, bits):
    count = lax.axis_size("expert")
    return lax.ppermute(value, "expert", [(k, k ^ bits) for k in range(count)])


def paired_local(tokens_in, out_grad, router_logits, expert_ids, saved_hidden, down_weight):
    flight = lax.axis_size("expert")
    cap, hidden = saved_hidden.shape[3:]
    tokens, width = out_grad.shape
    experts = router_logits.shape[1]
    half = hidden // 2
    slots = flight * cap
    f32, bf16 = jnp.float32, jnp.bfloat16
    dp, me = lax.axis_index("dp"), lax.axis_index("expert")
    place = jnp.stack([dp, me]).astype(jnp.int32)
    weight = down_weight[0]
    logits_t, ids_t = router_logits.T, expert_ids.T
    saved = saved_hidden.reshape(slots, hidden)

    ids_peer = over_expert(ids_t, 1)
    grad_peer = over_expert(out_grad, 1)
    saved_own = lax.dynamic_slice_in_dim(saved, dp * half, half, 1)
    saved_other = over_dp(lax.dynamic_slice_in_dim(saved, (1 - dp) * half, half, 1))

    bundle_rows = experts + 80
    z, a, bundle = kernel_call(
        lambda *refs: route_body(*refs, flight=flight),
        (
            jax.ShapeDtypeStruct((experts, tokens), f32),
            jax.ShapeDtypeStruct((experts, tokens), f32),
            jax.ShapeDtypeStruct((bundle_rows, tokens), bf16),
        ),
        "route", 1 << 22, 1 << 19, logits_t, ids_t,
    )
    blocks = kernel_call(
        lambda *refs: pack_body(*refs, cap=cap),
        tuple(jax.ShapeDtypeStruct((2 * cap, width), bf16) for _ in range(8)),
        "pack", 4 * slots * tokens * width, 3 << 20,
        place, ids_t, ids_peer, out_grad, grad_peer, smem=1,
    )
    own = [None] * 8
    own[0] = blocks[0]
    turn = [None] * 4
    for rz in (3, 2, 1):
        own[2 * rz] = over_expert(blocks[2 * rz], 4 * rz)
        turn[rz] = over_expert(blocks[2 * rz + 1], 2)
    own[1] = over_expert(blocks[1], 2)
    for rz in (3, 2, 1):
        own[2 * rz + 1] = over_expert(turn[rz], 4 * rz)
    other = [over_dp(piece) for piece in own]

    turned = kernel_call(
        turn_body, jax.ShapeDtypeStruct((width, tokens), bf16), "turn", 1 << 20, 2 << 20, tokens_in
    )
    turned = lax.all_to_all(
        turned.reshape(flight, width // flight, tokens), "expert", 0, 0, tiled=True
    )

    ring = jnp.stack([bundle] + [over_expert(bundle, 4 * rz) for rz in (1, 2, 3)])
    ring_y = over_expert(ring, 2)
    bundles = (ring, over_expert(ring, 1), ring_y, over_expert(ring_y, 1))

    grads_own, grads_other, gate_part = kernel_call(
        lambda *refs: grads_body(*refs, cap=cap),
        (
            jax.ShapeDtypeStruct((slots, half), f32),
            jax.ShapeDtypeStruct((slots, half), bf16),
            jax.ShapeDtypeStruct((2 * flight, 1, slots), f32),
        ),
        "grads", 4 * slots * width * half, 6 << 20,
        place, saved_own, saved_other, weight, *own, *other, smem=1,
    )
    gate_all = lax.all_to_all(gate_part, ("dp", "expert"), 0, 0, tiled=True)
    grads_back = over_dp(grads_other)
    hidden_grad = kernel_call(
        lambda *refs: hidden_body(*refs, cap=cap, experts=experts),
        jax.ShapeDtypeStruct((slots, hidden), bf16),
        "hidden", 1 << 24, 1 << 20,
        place, grads_own, grads_back, *bundles, smem=1,
    )
    logit_t, keep, send = kernel_call(
        lambda *refs: panel_body(*refs, cap=cap, experts=experts),
        (
            jax.ShapeDtypeStruct((experts, tokens), f32),
            jax.ShapeDtypeStruct((experts // 2, width // flight), f32),
            jax.ShapeDtypeStruct((experts // 2, width // flight), bf16),
        ),
        "panel", 1 << 28, 4 << 20,
        place, z, a, gate_all, turned, *bundles, smem=1,
    )
    router_t = keep + over_dp(send).astype(f32)
    return (
        hidden_grad.reshape(1, 1, flight, cap, hidden),
        logit_t.T,
        router_t.T,
    )


def solution(mesh):
    in_specs = (
        P(("dp", "expert"), None),
        P(("dp", "expert"), None),
        P(("dp", "expert"), None),
        P(("dp", "expert"), None),
        P("dp", "expert", None, None, None),
        P("expert", "dp", None),
    )
    out_specs = (P("dp", "expert", None, None, None), P(("dp", "expert"), None), P("expert", "dp"))
    paired = mesh.shape["dp"] == 2 and mesh.shape["expert"] == 16
    local = paired_local if paired else general_local
    return jax.shard_map(local, mesh=mesh, in_specs=in_specs, out_specs=out_specs, check_vma=False)
```

```python
import jax
import jax.numpy as jnp
from jax import lax
from jax.experimental import pallas as pl
from jax.experimental.pallas import tpu as pltpu
from jax.sharding import PartitionSpec as P

RSCALE = 2.827
ZLOSS = 0.25


def entering(shard, axis, combine, identity):
    length, place = (lax.axis_size(axis), lax.axis_index(axis))
    everything = lax.all_gather(shard.astype(jnp.bfloat16), axis)
    start = jnp.broadcast_to(jnp.asarray(identity, shard.dtype), shard.shape)

    def lap(k, before):
        reached = k < place
        new = combine(before, everything[k].astype(shard.dtype))
        return jnp.where(reached, new, before)

    return lax.fori_loop(0, length, lap, start)


def from_root(value, axis, source):
    kept = jnp.where(lax.axis_index(axis) == source, value, 0).astype(value.dtype)
    return lax.psum(kept, axis)


def slot_table(ids_block, flight, cap):
    owners = jnp.arange(flight, dtype=jnp.int32)
    chosen = jnp.any(ids_block[:, :, None] == owners[None, None, :], axis=1)
    as_int = chosen.astype(jnp.int32)
    rank = jnp.cumsum(as_int, axis=0) - as_int
    places = jnp.arange(cap, dtype=jnp.int32)
    table = chosen[None, :, :] & (rank[None, :, :] == places[:, None, None])
    return jnp.transpose(table, (2, 0, 1))


def own_columns(panel):
    count = panel.shape[1] // lax.axis_size("dp")
    return lax.dynamic_slice_in_dim(panel, lax.axis_index("dp") * count, count, 1)


def general_local(tokens_in, out_grad, router_logits, expert_ids, saved_hidden, down_weight):
    highest = lax.Precision.HIGHEST
    flight = lax.axis_size("expert")
    cap = saved_hidden.shape[3]
    hidden = saved_hidden.shape[4]
    width = out_grad.shape[1]
    experts = router_logits.shape[1]
    top = jnp.max(router_logits, axis=1, keepdims=True)
    shifted = jnp.exp(router_logits - top)
    total = jnp.sum(shifted, axis=1, keepdims=True)
    probs = shifted / total
    lse = top + jnp.log(total)
    columns = jnp.arange(experts, dtype=jnp.int32)
    picks = (expert_ids[:, :, None] == columns[None, None, :]).astype(jnp.float32)
    chosen_logit = jnp.sum(picks * router_logits[:, None, :], axis=2)
    scores = jax.nn.sigmoid(chosen_logit)
    ssum = jnp.sum(scores, axis=1, keepdims=True)
    gates = RSCALE * scores / ssum
    gate_half = gates.astype(jnp.bfloat16)
    in_window = picks[:, :, :flight]
    gate_te = jnp.sum(in_window * gate_half.astype(jnp.float32)[:, :, None], axis=1)
    table = slot_table(expert_ids, flight, cap)
    table_half = table.astype(jnp.bfloat16)
    table_full = table.astype(jnp.float32)
    send_rows = jnp.einsum(
        "ect,td->ecd", table_half, out_grad, preferred_element_type=jnp.float32
    ).astype(jnp.bfloat16)
    send_gates = jnp.einsum("ect,te->ec", table_full, gate_te, precision=highest).astype(
        jnp.bfloat16
    )
    recv_rows, recv_gates = (
        lax.all_to_all(send_rows, "expert", split_axis=0, concat_axis=0, tiled=True),
        lax.all_to_all(send_gates, "expert", split_axis=0, concat_axis=0, tiled=True),
    )
    flat_rows = recv_rows.reshape(flight * cap, width)
    part = lax.dot_general(
        flat_rows,
        lax.all_gather(down_weight, "dp", axis=1, tiled=True)[0],
        (((1,), (1,)), ((), ())),
        preferred_element_type=jnp.float32,
    )
    slot_gates = recv_gates.reshape(flight * cap, 1).astype(jnp.float32)
    hidden_grad = (slot_gates * part).astype(jnp.bfloat16).reshape(1, 1, flight, cap, hidden)
    saved_flat = saved_hidden.reshape(flight * cap, hidden)
    gate_grad = jnp.sum(saved_flat * part, axis=1).reshape(flight, cap)
    returned = lax.all_to_all(gate_grad, "expert", split_axis=0, concat_axis=0, tiled=True)
    grad_te = jnp.einsum("ect,ec->te", table_full, returned, precision=highest)
    grad_choice = jnp.sum(in_window * grad_te[:, None, :], axis=2)
    mixed = jnp.sum(grad_choice * gates, axis=1, keepdims=True) / RSCALE
    dscore = RSCALE / ssum * (grad_choice - mixed)
    dchosen = dscore * scores * (1.0 - scores)
    logit_grad = jnp.sum(picks * dchosen[:, :, None], axis=1) + 2.0 * ZLOSS * lse * probs
    tokens_full = tokens_in.astype(jnp.float32)
    own_rows = lax.psum_scatter(
        lax.dot_general(tokens_full, logit_grad, (((0,), (0,)), ((), ())), precision=highest),
        "expert",
        scatter_dimension=0,
        tiled=True,
    )
    before = entering(
        own_rows, "dp", lambda earlier, later: earlier + later, jnp.zeros_like(own_rows)
    )
    finished = before + own_rows
    spread = from_root(finished.astype(jnp.bfloat16), "dp", lax.axis_size("dp") - 1).astype(
        finished.dtype
    )
    router_grad = own_columns(spread)
    return (hidden_grad, logit_grad, router_grad)


NT = (((1,), (1,)), ((), ()))
NN = (((1,), (0,)), ((), ()))


def kernel_call(body, out_shape, name, flops, touched, *operands, far=(), scratch=(), room=24):
    def space(k, operand):
        if operand.shape == (2,):
            return pltpu.SMEM
        return pltpu.HBM if k in far else pltpu.VMEM

    return pl.pallas_call(
        body,
        out_shape=out_shape,
        in_specs=[pl.BlockSpec(memory_space=space(k, x)) for k, x in enumerate(operands)],
        out_specs=jax.tree.map(lambda _: pl.BlockSpec(memory_space=pltpu.VMEM), out_shape),
        scratch_shapes=scratch,
        compiler_params=pltpu.CompilerParams(vmem_limit_bytes=room * 1024 * 1024),
        cost_estimate=pl.CostEstimate(flops=flops, bytes_accessed=touched, transcendentals=0),
        name=name,
    )(*operands)


def iota(shape, dim):
    return lax.broadcasted_iota(jnp.int32, shape, dim)


def three_halves(value):
    high = value.astype(jnp.bfloat16)
    rest = value - high.astype(jnp.float32)
    middle = rest.astype(jnp.bfloat16)
    low = (rest - middle.astype(jnp.float32)).astype(jnp.bfloat16)
    return high, middle, low


def ranks(chosen):
    tokens = chosen.shape[1]
    before = (iota((tokens, tokens), 0) < iota((tokens, tokens), 1)).astype(jnp.bfloat16)
    return lax.dot_general(
        chosen.astype(jnp.bfloat16), before, NN, preferred_element_type=jnp.float32
    )


def first_body(place_ref, logits_ref, ids_ref, tokens_ref, saved_ref, *outs, flight, cap):
    z_ref, a_ref, gate_ref, saved_own_ref, saved_other_ref, *parcels, turned_ref = outs
    half = saved_own_ref.shape[1]
    for k, out in enumerate((saved_own_ref, saved_other_ref)):
        start = (place_ref[0] if k == 0 else 1 - place_ref[0]) * half
        out[...] = saved_ref[:, pl.ds(pl.multiple_of(start, 128), half)]
    logits = logits_ref[...]
    ids = ids_ref[...]
    experts, tokens = logits.shape
    topk = ids.shape[0]
    top = jnp.max(logits, axis=0, keepdims=True)
    shifted = jnp.exp(logits - top)
    total = jnp.sum(shifted, axis=0, keepdims=True)
    lse = top + jnp.log(total)
    z = (2.0 * ZLOSS) * lse * (shifted / total)
    z_ref[...] = z
    rows = iota((experts, tokens), 0)
    chosen = [
        jnp.sum(jnp.where(rows == ids[k : k + 1], logits, 0.0), axis=0, keepdims=True)
        for k in range(topk)
    ]
    scores = jax.nn.sigmoid(jnp.concatenate(chosen, axis=0))
    ssum = jnp.sum(scores, axis=0, keepdims=True)
    gates = RSCALE * scores / ssum
    slope = (RSCALE / ssum) * scores * (1.0 - scores)
    dense = jnp.zeros((experts, tokens), jnp.float32)
    window = iota((flight, tokens), 0)
    gate_te = jnp.zeros((flight, tokens), jnp.float32)
    picked = jnp.zeros((flight, tokens), jnp.float32)
    for k in range(topk):
        dense = jnp.where(rows == ids[k : k + 1], slope[k : k + 1], dense)
        gate_te = jnp.where(window == ids[k : k + 1], gates[k : k + 1], gate_te)
        picked = jnp.where(window == ids[k : k + 1], 1.0, picked)
    a_ref[...] = dense
    slot = jnp.where(picked > 0.0, ranks(picked), -1.0)
    high, middle, low = three_halves(gate_te)
    lanes = iota((flight, tokens), 1)
    slot_gates = jnp.zeros((flight, tokens), jnp.float32)
    for c in range(cap):
        here = jnp.sum(
            jnp.where(slot == float(c), high.astype(jnp.float32), 0.0), axis=1, keepdims=True
        )
        slot_gates = jnp.where(lanes == c, here, slot_gates)
    gate_ref[...] = slot_gates
    pairs = jnp.concatenate([ids.astype(jnp.float32), slope], axis=0).astype(jnp.bfloat16)
    parts = (z.astype(jnp.bfloat16), pairs, slot.astype(jnp.bfloat16), high, middle, low)
    bundle = jnp.concatenate(parts, axis=0)
    count = len(parcels)
    block = tokens_ref.shape[1] // flight
    turned_ref[...] = tokens_ref[...].T
    for j, parcel in enumerate(parcels):
        there = (place_ref[1] ^ j) & (count - 1)
        for h in range(2):
            start = pl.multiple_of((there + h * count) * block, 32)
            parcel[h * block : (h + 1) * block] = turned_ref[pl.ds(start, block)]
        parcel[2 * block : 2 * block + experts + 80] = bundle


def pack_body(place_ref, ids_ref, ids_peer_ref, out_grad_ref, out_grad_peer_ref, *outs, cap):
    me = place_ref[1]
    selects = []
    for ids_one in (ids_ref, ids_peer_ref):
        ids = ids_one[...]
        topk, tokens = ids.shape
        wanted = (iota((8, tokens), 0) * 2) ^ me
        picked = jnp.zeros((8, tokens), jnp.float32)
        for k in range(topk):
            picked = jnp.where(wanted == ids[k : k + 1], 1.0, picked)
        slot = jnp.where(picked > 0.0, ranks(picked), -1.0)
        place = iota((cap, tokens), 0).astype(jnp.float32)
        select = jnp.concatenate(
            [jnp.where(slot[q : q + 1] == place, 1.0, 0.0) for q in range(8)], axis=0
        )
        selects.append(select.astype(jnp.bfloat16))
    parts = [
        lax.dot_general(select, grad_one[...], NN, preferred_element_type=jnp.float32)
        for select, grad_one in zip(selects, (out_grad_ref, out_grad_peer_ref))
    ]
    for q, out in enumerate(outs):
        rows = slice(q * cap, (q + 1) * cap)
        out[...] = jnp.concatenate([parts[0][rows], parts[1][rows]], axis=0).astype(jnp.bfloat16)


def swap_matrix(me, size, cap, dtype):
    return (iota((size, size), 1) == (iota((size, size), 0) ^ (me * cap))).astype(dtype)


def finish_grads(me, grads, saved_ref, grads_ref, cap):
    slots = saved_ref.shape[0]
    swap = swap_matrix(me, slots, cap, jnp.bfloat16)
    where_to = swap_matrix(me, slots, cap, jnp.float32)
    saved = lax.dot_general(swap, saved_ref[...], NN, preferred_element_type=jnp.float32)
    grads_ref[...] = grads.astype(grads_ref.dtype)
    sums = jnp.sum(saved * grads, axis=1, keepdims=True)
    return jnp.sum(where_to * sums, axis=0, keepdims=True)


def grads_own_body(place_ref, saved_ref, weight_ref, *refs, cap):
    pieces, (grads_ref, line_ref) = refs[:8], refs[8:]
    rows = jnp.concatenate([p[...] for p in pieces], axis=0)
    grads = lax.dot_general(rows, weight_ref[...], NT, preferred_element_type=jnp.float32)
    line_ref[...] = finish_grads(place_ref[1], grads, saved_ref, grads_ref, cap)


def grads_other_body(place_ref, saved_ref, weight_ref, line_own_ref, gate_ref, *refs, cap):
    pieces, (grads_ref, message_ref) = refs[:8], refs[8:]
    rows = jnp.concatenate([p[...] for p in pieces], axis=0)
    grads = lax.dot_general(rows, weight_ref[...], NT, preferred_element_type=jnp.float32)
    other = finish_grads(place_ref[1], grads, saved_ref, grads_ref, cap)
    own = line_own_ref[...]
    dp = place_ref[0]
    count = message_ref.shape[0] // 2
    for k in range(2):
        line = jnp.where(dp == k, own, other)
        for e in range(count):
            message_ref[k * count + e] = jnp.concatenate([line, gate_ref[e : e + 1]], axis=0)


def hidden_body(place_ref, own_ref, other_ref, message_ref, out_ref, *, cap):
    dp, me = place_ref[0], place_ref[1]
    slots, half = own_ref.shape
    diagonal = iota((cap, slots), 0) == iota((cap, slots), 1)
    columns = []
    for r in range(16):
        line = message_ref[dp * 16 + (me ^ r), 1:2]
        columns.append(jnp.sum(jnp.where(diagonal, line, 0.0), axis=1, keepdims=True))
    gates = jnp.concatenate(columns, axis=0)
    swap = swap_matrix(me, slots, cap, jnp.bfloat16)
    for k, part in enumerate((own_ref, other_ref)):
        value = (gates * part[...].astype(jnp.float32)).astype(jnp.bfloat16)
        value = lax.dot_general(swap, value, NN, preferred_element_type=jnp.float32)
        start = pl.multiple_of((dp if k == 0 else 1 - dp) * half, 128)
        out_ref[:, pl.ds(start, half)] = value.astype(jnp.bfloat16)


def panel_body(place_ref, z_ref, a_ref, message_ref, *refs, cap):
    parcels, logit_ref, outs = refs[:8], refs[8], refs[9:]
    dp, me = place_ref[0], place_ref[1]
    experts, tokens = z_ref.shape
    sources = len(parcels)
    base = parcels[0].shape[0] - experts - 80
    gate_all = jnp.concatenate(
        [message_ref[e, 0:1] + message_ref[16 + e, 0:1] for e in range(16)], axis=0
    )
    upper = me >= sources
    swap = swap_matrix(me, gate_all.shape[1], cap, jnp.bfloat16)
    gate_rel = sum(
        lax.dot_general(part, swap, NN, preferred_element_type=jnp.float32)
        for part in three_halves(gate_all)
    )
    rows = iota((experts, tokens), 0).astype(jnp.float32)
    lines, blocks = [], []
    total = None
    for q, parcel_ref in enumerate(parcels):
        at = base + experts
        pairs = parcel_ref[at : at + 16].astype(jnp.float32)
        slot = parcel_ref[at + 16 : at + 32].astype(jnp.float32)
        gate = sum(
            parcel_ref[at + 32 + 16 * k : at + 48 + 16 * k].astype(jnp.float32)
            for k in (2, 1, 0)
        )
        grad = jnp.zeros((16, tokens), jnp.float32)
        for c in range(cap):
            grad = jnp.where(slot == float(c), gate_rel[:, q * cap + c : q * cap + c + 1], grad)
        mixed = jnp.sum(grad * gate, axis=0, keepdims=True) / RSCALE
        spread = jnp.concatenate(
            [grad - mixed, jnp.broadcast_to(-mixed, (experts - 16, tokens))], axis=0
        )
        if q == 0:
            logit_ref[...] = z_ref[...] + a_ref[...] * spread
        dense = jnp.zeros((experts, tokens), jnp.float32)
        for k in range(8):
            dense = jnp.where(rows == pairs[k : k + 1], pairs[8 + k : 9 + k], dense)
        line = parcel_ref[base:at].astype(jnp.float32) + dense * spread
        lines.append(line.astype(jnp.bfloat16))
        blocks.append(parcel_ref[:base])
        if len(lines) == 2:
            part = lax.dot_general(
                jnp.concatenate(lines, axis=1),
                jnp.concatenate(blocks, axis=1),
                NT,
                preferred_element_type=jnp.float32,
            )
            total = part if total is None else total + part
            lines, blocks = [], []
    columns, width = outs[0].shape
    for k, out in enumerate(outs):
        other_half, other_dp = k // 2, k % 2
        from_upper = upper if other_half == 0 else jnp.logical_not(upper)
        from_second = (dp == 1) if other_dp == 0 else (dp == 0)
        low = jnp.where(from_second, total[columns:, :width], total[:columns, :width])
        high = jnp.where(from_second, total[columns:, width:], total[:columns, width:])
        out[...] = jnp.where(from_upper, high, low).astype(out.dtype)


def over_dp(value):
    return lax.ppermute(value, "dp", [(0, 1), (1, 0)])


def over_expert(value, bits):
    count = lax.axis_size("expert")
    return lax.ppermute(value, "expert", [(k, k ^ bits) for k in range(count)])


def over_both(value, dp_bit, bits):
    count = lax.axis_size("expert")
    return lax.ppermute(
        value, ("dp", "expert"), [(k, k ^ (dp_bit * count + bits)) for k in range(2 * count)]
    )


def after(value, *earlier):
    return lax.optimization_barrier((value, *earlier))[0]


def paired_local(tokens_in, out_grad, router_logits, expert_ids, saved_hidden, down_weight):
    flight = lax.axis_size("expert")
    cap, hidden = saved_hidden.shape[3:]
    tokens, width = out_grad.shape
    experts = router_logits.shape[1]
    half, group = hidden // 2, flight // 2
    slots = flight * cap
    block = width // flight
    f32, bf16 = jnp.float32, jnp.bfloat16
    dp, me = lax.axis_index("dp"), lax.axis_index("expert")
    place = jnp.stack([dp, me]).astype(jnp.int32)
    weight = down_weight[0]
    logits_t, ids_t = router_logits.T, expert_ids.T
    saved = saved_hidden.reshape(slots, hidden)

    grad_peer = over_expert(out_grad, 1)
    ids_peer = over_expert(ids_t, 1)
    blocks = kernel_call(
        lambda *refs: pack_body(*refs, cap=cap),
        tuple(jax.ShapeDtypeStruct((2 * cap, width), bf16) for _ in range(8)),
        "pack", 4 * slots * tokens * width, 3 << 20,
        place, ids_t, ids_peer, out_grad, grad_peer,
    )
    logits_t, tokens_in, saved = after((logits_t, tokens_in, saved), blocks[0])
    z, a, slot_gates, saved_own, saved_other, *parcels = kernel_call(
        lambda *refs: first_body(*refs, flight=flight, cap=cap),
        (
            jax.ShapeDtypeStruct((experts, tokens), f32),
            jax.ShapeDtypeStruct((experts, tokens), f32),
            jax.ShapeDtypeStruct((flight, tokens), f32),
            jax.ShapeDtypeStruct((slots, half), bf16),
            jax.ShapeDtypeStruct((slots, half), bf16),
            *(jax.ShapeDtypeStruct((2 * block + experts + 80, tokens), bf16) for _ in range(group)),
        ),
        "first", 1 << 33, 3 << 20, place, logits_t, ids_t, tokens_in, saved,
        scratch=[pltpu.VMEM((width, tokens), bf16)],
    )
    own, other = [blocks[0]] + [None] * 7, [None] * 8
    sending = ((6, None), (1, None), (2, None), (7, 1), (3, 2), (4, 6), (5, 7))
    for q, gate in sending:
        piece = blocks[q] if gate is None else after(blocks[q], own[gate], slot_gates)
        own[q] = over_expert(piece, 2 * q)
    for q in range(8):
        other[q] = over_dp(own[q])
    saved_other = over_dp(saved_other)
    parcels = [parcels[0]] + [
        over_expert(after(parcels[j], own[4], own[7]), j) for j in range(1, group)
    ]
    grads_own, line_own = kernel_call(
        lambda *refs: grads_own_body(*refs, cap=cap),
        (jax.ShapeDtypeStruct((slots, half), f32), jax.ShapeDtypeStruct((1, slots), f32)),
        "grads_own", 40 * slots * width * half, 5 << 20, place, saved_own, weight, *own,
    )
    grads_other, message = kernel_call(
        lambda *refs: grads_other_body(*refs, cap=cap),
        (
            jax.ShapeDtypeStruct((slots, half), bf16),
            jax.ShapeDtypeStruct((2 * flight, 2, slots), f32),
        ),
        "grads_other", 40 * slots * width * half, 5 << 20,
        place, saved_other, weight, line_own, slot_gates, *other,
    )
    grads_back = over_dp(grads_other)
    message = lax.all_to_all(message, ("dp", "expert"), 0, 0, tiled=True)
    message, grads_back = lax.optimization_barrier((message, grads_back))
    logit_t, *sums = kernel_call(
        lambda *refs: panel_body(*refs, cap=cap),
        (
            jax.ShapeDtypeStruct((experts, tokens), f32),
            jax.ShapeDtypeStruct((experts // 2, block), f32),
            *(jax.ShapeDtypeStruct((experts // 2, block), bf16) for _ in range(3)),
        ),
        "panel", 1 << 28, 4 << 20,
        place, z, a, message, *parcels,
    )
    hidden_grad = kernel_call(
        lambda *refs: hidden_body(*refs, cap=cap),
        jax.ShapeDtypeStruct((slots, hidden), bf16),
        "hidden", 1 << 24, 1 << 20,
        place, grads_own, grads_back, message,
    )
    far = [over_both(sums[3], 1, group), over_both(sums[2], 0, group), over_both(sums[1], 1, 0)]
    router_t = after(sums[0], hidden_grad) + sum(part.astype(f32) for part in far)
    return (
        hidden_grad.reshape(1, 1, flight, cap, hidden),
        logit_t.T,
        router_t.T,
    )


def solution(mesh):
    in_specs = (
        P(("dp", "expert"), None),
        P(("dp", "expert"), None),
        P(("dp", "expert"), None),
        P(("dp", "expert"), None),
        P("dp", "expert", None, None, None),
        P("expert", "dp", None),
    )
    out_specs = (P("dp", "expert", None, None, None), P(("dp", "expert"), None), P("expert", "dp"))
    paired = mesh.shape["dp"] == 2 and mesh.shape["expert"] == 16
    local = paired_local if paired else general_local
    return jax.shard_map(local, mesh=mesh, in_specs=in_specs, out_specs=out_specs, check_vma=False)
```

```python
import jax
import jax.numpy as jnp
from jax import lax
from jax.experimental import pallas as pl
from jax.experimental.pallas import tpu as pltpu
from jax.sharding import PartitionSpec as P

RSCALE = 2.827
ZLOSS = 0.25


def entering(shard, axis, combine, identity):
    length, place = (lax.axis_size(axis), lax.axis_index(axis))
    everything = lax.all_gather(shard.astype(jnp.bfloat16), axis)
    start = jnp.broadcast_to(jnp.asarray(identity, shard.dtype), shard.shape)

    def lap(k, before):
        reached = k < place
        new = combine(before, everything[k].astype(shard.dtype))
        return jnp.where(reached, new, before)

    return lax.fori_loop(0, length, lap, start)


def from_root(value, axis, source):
    kept = jnp.where(lax.axis_index(axis) == source, value, 0).astype(value.dtype)
    return lax.psum(kept, axis)


def slot_table(ids_block, flight, cap):
    owners = jnp.arange(flight, dtype=jnp.int32)
    chosen = jnp.any(ids_block[:, :, None] == owners[None, None, :], axis=1)
    as_int = chosen.astype(jnp.int32)
    rank = jnp.cumsum(as_int, axis=0) - as_int
    places = jnp.arange(cap, dtype=jnp.int32)
    table = chosen[None, :, :] & (rank[None, :, :] == places[:, None, None])
    return jnp.transpose(table, (2, 0, 1))


def own_columns(panel):
    count = panel.shape[1] // lax.axis_size("dp")
    return lax.dynamic_slice_in_dim(panel, lax.axis_index("dp") * count, count, 1)


def general_local(tokens_in, out_grad, router_logits, expert_ids, saved_hidden, down_weight):
    highest = lax.Precision.HIGHEST
    flight = lax.axis_size("expert")
    cap = saved_hidden.shape[3]
    hidden = saved_hidden.shape[4]
    width = out_grad.shape[1]
    experts = router_logits.shape[1]
    top = jnp.max(router_logits, axis=1, keepdims=True)
    shifted = jnp.exp(router_logits - top)
    total = jnp.sum(shifted, axis=1, keepdims=True)
    probs = shifted / total
    lse = top + jnp.log(total)
    columns = jnp.arange(experts, dtype=jnp.int32)
    picks = (expert_ids[:, :, None] == columns[None, None, :]).astype(jnp.float32)
    chosen_logit = jnp.sum(picks * router_logits[:, None, :], axis=2)
    scores = jax.nn.sigmoid(chosen_logit)
    ssum = jnp.sum(scores, axis=1, keepdims=True)
    gates = RSCALE * scores / ssum
    gate_half = gates.astype(jnp.bfloat16)
    in_window = picks[:, :, :flight]
    gate_te = jnp.sum(in_window * gate_half.astype(jnp.float32)[:, :, None], axis=1)
    table = slot_table(expert_ids, flight, cap)
    table_half = table.astype(jnp.bfloat16)
    table_full = table.astype(jnp.float32)
    send_rows = jnp.einsum(
        "ect,td->ecd", table_half, out_grad, preferred_element_type=jnp.float32
    ).astype(jnp.bfloat16)
    send_gates = jnp.einsum("ect,te->ec", table_full, gate_te, precision=highest).astype(
        jnp.bfloat16
    )
    recv_rows, recv_gates = (
        lax.all_to_all(send_rows, "expert", split_axis=0, concat_axis=0, tiled=True),
        lax.all_to_all(send_gates, "expert", split_axis=0, concat_axis=0, tiled=True),
    )
    flat_rows = recv_rows.reshape(flight * cap, width)
    part = lax.dot_general(
        flat_rows,
        lax.all_gather(down_weight, "dp", axis=1, tiled=True)[0],
        (((1,), (1,)), ((), ())),
        preferred_element_type=jnp.float32,
    )
    slot_gates = recv_gates.reshape(flight * cap, 1).astype(jnp.float32)
    hidden_grad = (slot_gates * part).astype(jnp.bfloat16).reshape(1, 1, flight, cap, hidden)
    saved_flat = saved_hidden.reshape(flight * cap, hidden)
    gate_grad = jnp.sum(saved_flat * part, axis=1).reshape(flight, cap)
    returned = lax.all_to_all(gate_grad, "expert", split_axis=0, concat_axis=0, tiled=True)
    grad_te = jnp.einsum("ect,ec->te", table_full, returned, precision=highest)
    grad_choice = jnp.sum(in_window * grad_te[:, None, :], axis=2)
    mixed = jnp.sum(grad_choice * gates, axis=1, keepdims=True) / RSCALE
    dscore = RSCALE / ssum * (grad_choice - mixed)
    dchosen = dscore * scores * (1.0 - scores)
    logit_grad = jnp.sum(picks * dchosen[:, :, None], axis=1) + 2.0 * ZLOSS * lse * probs
    tokens_full = tokens_in.astype(jnp.float32)
    own_rows = lax.psum_scatter(
        lax.dot_general(tokens_full, logit_grad, (((0,), (0,)), ((), ())), precision=highest),
        "expert",
        scatter_dimension=0,
        tiled=True,
    )
    before = entering(
        own_rows, "dp", lambda earlier, later: earlier + later, jnp.zeros_like(own_rows)
    )
    finished = before + own_rows
    spread = from_root(finished.astype(jnp.bfloat16), "dp", lax.axis_size("dp") - 1).astype(
        finished.dtype
    )
    router_grad = own_columns(spread)
    return (hidden_grad, logit_grad, router_grad)


HINT = {
    "pack_own": 1 << 28, "pack": 1 << 28, "first": 1 << 33, "join": 1 << 20, "merge": 1 << 10,
    "grads_own": 40 << 28, "grads_other": 400 << 28, "prepare": 1 << 33, "panel": 1 << 28,
    "hidden": 1 << 24,
}
ORDER = (
    ("send", 0), ("forward", (0,)), ("send", 6), ("send", 1), ("send", 2), ("send", 7), ("send", 3),
    ("forward", (1,)), ("forward", (2,)), ("send", 4), ("first", 0), ("send", 5), ("forward", (3,)),
    ("forward", (6,)), ("forward", (7,)), ("forward", (4,)), ("forward", (5,)),
)
SEND = {
    7: (("own", 1),), 3: (("own", 2), ("other", 0)), 4: (("own", 6), ("other", 0)),
    5: (("own", 7), ("other", 1), ("first", 0)),
}
FORWARD = {}
FIRST = (("block", 0),)
SAVED = ()
MERGE = (("own", 5),)


NT = (((1,), (1,)), ((), ()))
NN = (((1,), (0,)), ((), ()))


def kernel_call(body, out_shape, name, flops, touched, *operands, far=(), scratch=(), room=24):
    def space(k, operand):
        if operand.shape == (2,):
            return pltpu.SMEM
        return pltpu.HBM if k in far else pltpu.VMEM

    return pl.pallas_call(
        body,
        out_shape=out_shape,
        in_specs=[pl.BlockSpec(memory_space=space(k, x)) for k, x in enumerate(operands)],
        out_specs=jax.tree.map(lambda _: pl.BlockSpec(memory_space=pltpu.VMEM), out_shape),
        scratch_shapes=scratch,
        compiler_params=pltpu.CompilerParams(vmem_limit_bytes=room * 1024 * 1024),
        cost_estimate=pl.CostEstimate(flops=flops, bytes_accessed=touched, transcendentals=0),
        name=name,
    )(*operands)


def iota(shape, dim):
    return lax.broadcasted_iota(jnp.int32, shape, dim)


def three_halves(value):
    high = value.astype(jnp.bfloat16)
    rest = value - high.astype(jnp.float32)
    middle = rest.astype(jnp.bfloat16)
    low = (rest - middle.astype(jnp.float32)).astype(jnp.bfloat16)
    return high, middle, low


def ranks(chosen):
    tokens = chosen.shape[1]
    before = (iota((tokens, tokens), 0) < iota((tokens, tokens), 1)).astype(jnp.bfloat16)
    return lax.dot_general(
        chosen.astype(jnp.bfloat16), before, NN, preferred_element_type=jnp.float32
    )


def first_body(place_ref, logits_ref, ids_ref, tokens_ref, saved_ref, *outs, flight, cap):
    z_ref, a_ref, gate_ref, saved_own_ref, saved_other_ref, keep_ref, send_ref, turned_ref = outs
    half = saved_own_ref.shape[1]
    for k, out in enumerate((saved_own_ref, saved_other_ref)):
        start = (place_ref[0] if k == 0 else 1 - place_ref[0]) * half
        out[...] = saved_ref[:, pl.ds(pl.multiple_of(start, 128), half)]
    logits = logits_ref[...]
    ids = ids_ref[...]
    experts, tokens = logits.shape
    topk = ids.shape[0]
    top = jnp.max(logits, axis=0, keepdims=True)
    shifted = jnp.exp(logits - top)
    total = jnp.sum(shifted, axis=0, keepdims=True)
    lse = top + jnp.log(total)
    z = (2.0 * ZLOSS) * lse * (shifted / total)
    z_ref[...] = z
    rows = iota((experts, tokens), 0)
    chosen = [
        jnp.sum(jnp.where(rows == ids[k : k + 1], logits, 0.0), axis=0, keepdims=True)
        for k in range(topk)
    ]
    scores = jax.nn.sigmoid(jnp.concatenate(chosen, axis=0))
    ssum = jnp.sum(scores, axis=0, keepdims=True)
    gates = RSCALE * scores / ssum
    slope = (RSCALE / ssum) * scores * (1.0 - scores)
    dense = jnp.zeros((experts, tokens), jnp.float32)
    window = iota((flight, tokens), 0)
    gate_te = jnp.zeros((flight, tokens), jnp.float32)
    picked = jnp.zeros((flight, tokens), jnp.float32)
    for k in range(topk):
        dense = jnp.where(rows == ids[k : k + 1], slope[k : k + 1], dense)
        gate_te = jnp.where(window == ids[k : k + 1], gates[k : k + 1], gate_te)
        picked = jnp.where(window == ids[k : k + 1], 1.0, picked)
    a_ref[...] = dense
    slot = jnp.where(picked > 0.0, ranks(picked), -1.0)
    high, middle, low = three_halves(gate_te)
    lanes = iota((flight, tokens), 1)
    slot_gates = jnp.zeros((flight, tokens), jnp.float32)
    for c in range(cap):
        here = jnp.sum(
            jnp.where(slot == float(c), high.astype(jnp.float32), 0.0), axis=1, keepdims=True
        )
        slot_gates = jnp.where(lanes == c, here, slot_gates)
    gate_ref[...] = slot_gates
    pairs = jnp.concatenate([ids.astype(jnp.float32), slope], axis=0).astype(jnp.bfloat16)
    parts = (z.astype(jnp.bfloat16), pairs, slot.astype(jnp.bfloat16), high, middle, low)
    bundle = jnp.concatenate(parts, axis=0)
    count = 2 * keep_ref.shape[0]
    block = tokens_ref.shape[1] // flight
    turned_ref[...] = tokens_ref[...].T
    for j in range(count):
        parcel = (keep_ref, send_ref)[j % 2]
        there = (place_ref[1] ^ j) & (count - 1)
        for h in range(2):
            start = pl.multiple_of((there + h * count) * block, 32)
            parcel[j // 2, h * block : (h + 1) * block] = turned_ref[pl.ds(start, block)]
        parcel[j // 2, 2 * block : 2 * block + experts + 80] = bundle


def merge_body(keep_ref, got_ref, *outs):
    for q, out in enumerate(outs):
        out[0] = keep_ref[q + 1]
        out[1] = got_ref[q + 1]


def pack_one(me, ids, grad, cap):
    topk, tokens = ids.shape
    wanted = (iota((8, tokens), 0) * 2) ^ me
    picked = jnp.zeros((8, tokens), jnp.float32)
    for k in range(topk):
        picked = jnp.where(wanted == ids[k : k + 1], 1.0, picked)
    slot = jnp.where(picked > 0.0, ranks(picked), -1.0)
    place = iota((cap, tokens), 0).astype(jnp.float32)
    select = jnp.concatenate(
        [jnp.where(slot[q : q + 1] == place, 1.0, 0.0) for q in range(8)], axis=0
    )
    return lax.dot_general(
        select.astype(jnp.bfloat16), grad, NN, preferred_element_type=jnp.float32
    )


def pack_own_body(place_ref, ids_ref, grad_ref, out_ref, *, cap):
    out_ref[...] = pack_one(place_ref[1], ids_ref[...], grad_ref[...], cap)


def pack_body(place_ref, own_ref, ids_ref, grad_ref, *outs, cap):
    peer = pack_one(place_ref[1], ids_ref[...], grad_ref[...], cap)
    for q, out in enumerate(outs):
        rows = slice(q * cap, (q + 1) * cap)
        out[...] = jnp.concatenate([own_ref[rows], peer[rows]], axis=0).astype(jnp.bfloat16)


def swap_matrix(me, size, cap, dtype):
    return (iota((size, size), 1) == (iota((size, size), 0) ^ (me * cap))).astype(dtype)


def finish_grads(me, grads, saved_ref, grads_ref, cap):
    slots = saved_ref.shape[0]
    swap = swap_matrix(me, slots, cap, jnp.bfloat16)
    where_to = swap_matrix(me, slots, cap, jnp.float32)
    saved = lax.dot_general(swap, saved_ref[...], NN, preferred_element_type=jnp.float32)
    grads_ref[...] = grads.astype(grads_ref.dtype)
    sums = jnp.sum(saved * grads, axis=1, keepdims=True)
    return jnp.sum(where_to * sums, axis=0, keepdims=True)


def grads_own_body(place_ref, saved_ref, weight_ref, *refs, cap):
    pieces, (grads_ref, line_ref) = refs[:-2], refs[-2:]
    rows = jnp.concatenate([p[...] for p in pieces], axis=0)
    grads = lax.dot_general(rows, weight_ref[...], NT, preferred_element_type=jnp.float32)
    line_ref[...] = finish_grads(place_ref[1], grads, saved_ref, grads_ref, cap)


def grads_other_body(place_ref, saved_ref, weight_ref, line_own_ref, gate_ref, *refs, cap):
    pieces, (grads_ref, message_ref) = refs[:-2], refs[-2:]
    rows = jnp.concatenate([p[...] for p in pieces], axis=0)
    grads = lax.dot_general(rows, weight_ref[...], NT, preferred_element_type=jnp.float32)
    other = finish_grads(place_ref[1], grads, saved_ref, grads_ref, cap)
    own = line_own_ref[...]
    dp = place_ref[0]
    count = message_ref.shape[0] // 2
    for k in range(2):
        line = jnp.where(dp == k, own, other)
        for e in range(count):
            message_ref[k * count + e] = jnp.concatenate([line, gate_ref[e : e + 1]], axis=0)


def hidden_body(place_ref, own_ref, other_ref, message_ref, out_ref, *, cap):
    dp, me = place_ref[0], place_ref[1]
    slots, half = own_ref.shape
    diagonal = iota((cap, slots), 0) == iota((cap, slots), 1)
    columns = []
    for r in range(16):
        line = message_ref[dp * 16 + (me ^ r), 1:2]
        columns.append(jnp.sum(jnp.where(diagonal, line, 0.0), axis=1, keepdims=True))
    gates = jnp.concatenate(columns, axis=0)
    swap = swap_matrix(me, slots, cap, jnp.bfloat16)
    for k, part in enumerate((own_ref, other_ref)):
        value = (gates * part[...].astype(jnp.float32)).astype(jnp.bfloat16)
        value = lax.dot_general(swap, value, NN, preferred_element_type=jnp.float32)
        start = pl.multiple_of((dp if k == 0 else 1 - dp) * half, 128)
        out_ref[:, pl.ds(start, half)] = value.astype(jnp.bfloat16)


def views(parcels):
    return [(parcels[0], 0), (parcels[1], 0)] + [(p, k) for p in parcels[2:] for k in range(2)]


def prepare_body(*refs, experts):
    parcels, (dense_ref, gate_ref) = refs[:5], refs[5:]
    tokens = dense_ref.shape[2]
    at = parcels[0].shape[1] - 80
    rows = iota((experts, tokens), 0).astype(jnp.float32)
    for q, (parcel, here) in enumerate(views(parcels)):
        pairs = parcel[here, at : at + 16].astype(jnp.float32)
        dense = jnp.zeros((experts, tokens), jnp.float32)
        for k in range(8):
            dense = jnp.where(rows == pairs[k : k + 1], pairs[8 + k : 9 + k], dense)
        dense_ref[q] = dense
        gate_ref[q] = sum(
            parcel[here, at + 32 + 16 * k : at + 48 + 16 * k].astype(jnp.float32)
            for k in (2, 1, 0)
        )


def panel_body(place_ref, z_ref, a_ref, message_ref, dense_ref, gate_ref, *refs, cap):
    parcels, logit_ref, outs = refs[:5], refs[5], refs[6:]
    dp, me = place_ref[0], place_ref[1]
    experts, tokens = z_ref.shape
    base = parcels[0].shape[1] - experts - 80
    at = base + experts
    gate_all = jnp.concatenate(
        [message_ref[e, 0:1] + message_ref[16 + e, 0:1] for e in range(16)], axis=0
    )
    swap = swap_matrix(me, gate_all.shape[1], cap, jnp.bfloat16)
    gate_rel = sum(
        lax.dot_general(part, swap, NN, preferred_element_type=jnp.float32)
        for part in three_halves(gate_all)
    )
    lines, blocks = [], []
    total = None
    for q, (parcel, here) in enumerate(views(parcels)):
        slot = parcel[here, at + 16 : at + 32].astype(jnp.float32)
        grad = jnp.zeros((16, tokens), jnp.float32)
        for c in range(cap):
            grad = jnp.where(slot == float(c), gate_rel[:, q * cap + c : q * cap + c + 1], grad)
        mixed = jnp.sum(grad * gate_ref[q], axis=0, keepdims=True) / RSCALE
        spread = jnp.concatenate(
            [grad - mixed, jnp.broadcast_to(-mixed, (experts - 16, tokens))], axis=0
        )
        if q == 0:
            logit_ref[...] = z_ref[...] + a_ref[...] * spread
        line = parcel[here, base:at].astype(jnp.float32) + dense_ref[q] * spread
        lines.append(line.astype(jnp.bfloat16))
        blocks.append(parcel[here, :base])
        if len(lines) == 2:
            part = lax.dot_general(
                jnp.concatenate(lines, axis=1),
                jnp.concatenate(blocks, axis=1),
                NT,
                preferred_element_type=jnp.float32,
            )
            total = part if total is None else total + part
            lines, blocks = [], []
    upper = me >= len(views(parcels))
    columns, width = outs[0].shape
    for k, out in enumerate(outs):
        other_half, other_dp = k // 2, k % 2
        from_upper = upper if other_half == 0 else jnp.logical_not(upper)
        from_second = (dp == 1) if other_dp == 0 else (dp == 0)
        low = jnp.where(from_second, total[columns:, :width], total[:columns, :width])
        high = jnp.where(from_second, total[columns:, width:], total[:columns, width:])
        out[...] = jnp.where(from_upper, high, low).astype(out.dtype)


def join_body(*refs):
    refs[-1][...] = jnp.concatenate([ref[...] for ref in refs[:-1]], axis=0)


def over_dp(value):
    return lax.ppermute(value, "dp", [(0, 1), (1, 0)])


def over_expert(value, bits):
    count = lax.axis_size("expert")
    return lax.ppermute(value, "expert", [(k, k ^ bits) for k in range(count)])


def over_both(value, dp_bit, bits):
    count = lax.axis_size("expert")
    return lax.ppermute(
        value, ("dp", "expert"), [(k, k ^ (dp_bit * count + bits)) for k in range(2 * count)]
    )


def after(value, *earlier):
    return lax.optimization_barrier((value, *earlier))[0]


def paired_local(tokens_in, out_grad, router_logits, expert_ids, saved_hidden, down_weight):
    flight = lax.axis_size("expert")
    cap, hidden = saved_hidden.shape[3:]
    tokens, width = out_grad.shape
    experts = router_logits.shape[1]
    half, group = hidden // 2, flight // 2
    slots = flight * cap
    block = width // flight
    f32, bf16 = jnp.float32, jnp.bfloat16
    dp, me = lax.axis_index("dp"), lax.axis_index("expert")
    place = jnp.stack([dp, me]).astype(jnp.int32)
    weight = down_weight[0]
    logits_t, ids_t = router_logits.T, expert_ids.T
    saved = saved_hidden.reshape(slots, hidden)

    grad_peer = over_expert(out_grad, 1)
    ids_peer = over_expert(ids_t, 1)
    packed = kernel_call(
        lambda *refs: pack_own_body(*refs, cap=cap),
        jax.ShapeDtypeStruct((slots // 2, width), f32),
        "pack_own", HINT["pack_own"], 3 << 20, place, ids_t, out_grad,
    )
    blocks = kernel_call(
        lambda *refs: pack_body(*refs, cap=cap),
        tuple(jax.ShapeDtypeStruct((2 * cap, width), bf16) for _ in range(8)),
        "pack", HINT["pack"], 3 << 20, place, packed, ids_peer, grad_peer,
    )
    known = {("block", 0): blocks[0]}

    def parcel_shape(count):
        return jax.ShapeDtypeStruct((count, 2 * block + experts + 80, tokens), bf16)

    def held(value, waits):
        return after(value, *(known[w] for w in waits)) if waits else value

    def send(q):
        known["own", q] = over_expert(held(blocks[q], SEND.get(q, ())), 2 * q) if q else blocks[0]

    def forward(group):
        pieces = [known["own", q] for q in group]
        if len(pieces) > 1:
            pieces = [
                kernel_call(
                    join_body,
                    jax.ShapeDtypeStruct((2 * cap * len(pieces), width), bf16),
                    "join", HINT["join"], 1 << 20, *pieces,
                )
            ]
        known["other", group[0]] = over_dp(held(pieces[0], FORWARD.get(group[0], ())))

    def first():
        nonlocal logits_t, tokens_in, saved
        logits_t, tokens_in, saved = held((logits_t, tokens_in, saved), FIRST)
        outs = kernel_call(
            lambda *refs: first_body(*refs, flight=flight, cap=cap),
            (
                jax.ShapeDtypeStruct((experts, tokens), f32),
                jax.ShapeDtypeStruct((experts, tokens), f32),
                jax.ShapeDtypeStruct((flight, tokens), f32),
                jax.ShapeDtypeStruct((slots, half), bf16),
                jax.ShapeDtypeStruct((slots, half), bf16),
                *(parcel_shape(group // 2),) * 2,
            ),
            "first", HINT["first"], 3 << 20, place, logits_t, ids_t, tokens_in, saved,
            scratch=[pltpu.VMEM((width, tokens), bf16)],
        )
        known["first", 0] = outs[2]
        known["results", 0] = outs

    for kind, which in ORDER:
        {"send": send, "forward": forward, "first": lambda _: first()}[kind](which)
    z, a, slot_gates, saved_own, saved_other, parcel_keep, parcel_send = known["results", 0]
    own = [known["own", q] for q in range(8)]
    groups = [which for kind, which in ORDER if kind == "forward"]
    arrival = [q for members in sorted(groups) for q in members]
    other = [known["other", members[0]] for members in sorted(groups)]
    assert arrival == list(range(8))
    saved_other = over_dp(held(saved_other, SAVED))
    parcel_got = over_expert(parcel_send, 1)
    merged = kernel_call(
        merge_body, (parcel_shape(2),) * 3, "merge", HINT["merge"], 4 << 20,
        held(parcel_keep, MERGE), parcel_got,
    )
    parcels = (parcel_keep, parcel_got, *(over_expert(m, 2 * q + 2) for q, m in enumerate(merged)))
    grads_own, line_own = kernel_call(
        lambda *refs: grads_own_body(*refs, cap=cap),
        (jax.ShapeDtypeStruct((slots, half), f32), jax.ShapeDtypeStruct((1, slots), f32)),
        "grads_own", HINT["grads_own"], 5 << 20, place, saved_own, weight, *own,
    )
    grads_other, message = kernel_call(
        lambda *refs: grads_other_body(*refs, cap=cap),
        (
            jax.ShapeDtypeStruct((slots, half), bf16),
            jax.ShapeDtypeStruct((2 * flight, 2, slots), f32),
        ),
        "grads_other", HINT["grads_other"], 5 << 20,
        place, saved_other, weight, line_own, slot_gates, *other,
    )
    grads_back = over_dp(grads_other)
    message = lax.all_to_all(message, ("dp", "expert"), 0, 0, tiled=True)
    message, grads_back = lax.optimization_barrier((message, grads_back))
    dense, gates = kernel_call(
        lambda *refs: prepare_body(*refs, experts=experts),
        (
            jax.ShapeDtypeStruct((group, experts, tokens), f32),
            jax.ShapeDtypeStruct((group, 16, tokens), f32),
        ),
        "prepare", HINT["prepare"], 1 << 20, *parcels,
    )
    logit_t, *sums = kernel_call(
        lambda *refs: panel_body(*refs, cap=cap),
        (
            jax.ShapeDtypeStruct((experts, tokens), f32),
            jax.ShapeDtypeStruct((experts // 2, block), f32),
            *(jax.ShapeDtypeStruct((experts // 2, block), bf16) for _ in range(3)),
        ),
        "panel", HINT["panel"], 4 << 20,
        place, z, a, message, dense, gates, *parcels,
    )
    hidden_grad = kernel_call(
        lambda *refs: hidden_body(*refs, cap=cap),
        jax.ShapeDtypeStruct((slots, hidden), bf16),
        "hidden", HINT["hidden"], 1 << 20,
        place, grads_own, grads_back, message,
    )
    far = [over_both(sums[3], 1, group), over_both(sums[2], 0, group), over_both(sums[1], 1, 0)]
    router_t = after(sums[0], hidden_grad) + sum(part.astype(f32) for part in far)
    return (
        hidden_grad.reshape(1, 1, flight, cap, hidden),
        logit_t.T,
        router_t.T,
    )


def solution(mesh):
    in_specs = (
        P(("dp", "expert"), None),
        P(("dp", "expert"), None),
        P(("dp", "expert"), None),
        P(("dp", "expert"), None),
        P("dp", "expert", None, None, None),
        P("expert", "dp", None),
    )
    out_specs = (P("dp", "expert", None, None, None), P(("dp", "expert"), None), P("expert", "dp"))
    paired = mesh.shape["dp"] == 2 and mesh.shape["expert"] == 16
    local = paired_local if paired else general_local
    return jax.shard_map(local, mesh=mesh, in_specs=in_specs, out_specs=out_specs, check_vma=False)
```

```python
import jax
import jax.numpy as jnp
from jax import lax
from jax.experimental import pallas as pl
from jax.experimental.pallas import tpu as pltpu
from jax.sharding import PartitionSpec as P

RSCALE = 2.827
ZLOSS = 0.25


def entering(shard, axis, combine, identity):
    length, place = (lax.axis_size(axis), lax.axis_index(axis))
    everything = lax.all_gather(shard.astype(jnp.bfloat16), axis)
    start = jnp.broadcast_to(jnp.asarray(identity, shard.dtype), shard.shape)

    def lap(k, before):
        reached = k < place
        new = combine(before, everything[k].astype(shard.dtype))
        return jnp.where(reached, new, before)

    return lax.fori_loop(0, length, lap, start)


def from_root(value, axis, source):
    kept = jnp.where(lax.axis_index(axis) == source, value, 0).astype(value.dtype)
    return lax.psum(kept, axis)


def slot_table(ids_block, flight, cap):
    owners = jnp.arange(flight, dtype=jnp.int32)
    chosen = jnp.any(ids_block[:, :, None] == owners[None, None, :], axis=1)
    as_int = chosen.astype(jnp.int32)
    rank = jnp.cumsum(as_int, axis=0) - as_int
    places = jnp.arange(cap, dtype=jnp.int32)
    table = chosen[None, :, :] & (rank[None, :, :] == places[:, None, None])
    return jnp.transpose(table, (2, 0, 1))


def own_columns(panel):
    count = panel.shape[1] // lax.axis_size("dp")
    return lax.dynamic_slice_in_dim(panel, lax.axis_index("dp") * count, count, 1)


def general_local(tokens_in, out_grad, router_logits, expert_ids, saved_hidden, down_weight):
    highest = lax.Precision.HIGHEST
    flight = lax.axis_size("expert")
    cap = saved_hidden.shape[3]
    hidden = saved_hidden.shape[4]
    width = out_grad.shape[1]
    experts = router_logits.shape[1]
    top = jnp.max(router_logits, axis=1, keepdims=True)
    shifted = jnp.exp(router_logits - top)
    total = jnp.sum(shifted, axis=1, keepdims=True)
    probs = shifted / total
    lse = top + jnp.log(total)
    columns = jnp.arange(experts, dtype=jnp.int32)
    picks = (expert_ids[:, :, None] == columns[None, None, :]).astype(jnp.float32)
    chosen_logit = jnp.sum(picks * router_logits[:, None, :], axis=2)
    scores = jax.nn.sigmoid(chosen_logit)
    ssum = jnp.sum(scores, axis=1, keepdims=True)
    gates = RSCALE * scores / ssum
    gate_half = gates.astype(jnp.bfloat16)
    in_window = picks[:, :, :flight]
    gate_te = jnp.sum(in_window * gate_half.astype(jnp.float32)[:, :, None], axis=1)
    table = slot_table(expert_ids, flight, cap)
    table_half = table.astype(jnp.bfloat16)
    table_full = table.astype(jnp.float32)
    send_rows = jnp.einsum(
        "ect,td->ecd", table_half, out_grad, preferred_element_type=jnp.float32
    ).astype(jnp.bfloat16)
    send_gates = jnp.einsum("ect,te->ec", table_full, gate_te, precision=highest).astype(
        jnp.bfloat16
    )
    recv_rows, recv_gates = (
        lax.all_to_all(send_rows, "expert", split_axis=0, concat_axis=0, tiled=True),
        lax.all_to_all(send_gates, "expert", split_axis=0, concat_axis=0, tiled=True),
    )
    flat_rows = recv_rows.reshape(flight * cap, width)
    part = lax.dot_general(
        flat_rows,
        lax.all_gather(down_weight, "dp", axis=1, tiled=True)[0],
        (((1,), (1,)), ((), ())),
        preferred_element_type=jnp.float32,
    )
    slot_gates = recv_gates.reshape(flight * cap, 1).astype(jnp.float32)
    hidden_grad = (slot_gates * part).astype(jnp.bfloat16).reshape(1, 1, flight, cap, hidden)
    saved_flat = saved_hidden.reshape(flight * cap, hidden)
    gate_grad = jnp.sum(saved_flat * part, axis=1).reshape(flight, cap)
    returned = lax.all_to_all(gate_grad, "expert", split_axis=0, concat_axis=0, tiled=True)
    grad_te = jnp.einsum("ect,ec->te", table_full, returned, precision=highest)
    grad_choice = jnp.sum(in_window * grad_te[:, None, :], axis=2)
    mixed = jnp.sum(grad_choice * gates, axis=1, keepdims=True) / RSCALE
    dscore = RSCALE / ssum * (grad_choice - mixed)
    dchosen = dscore * scores * (1.0 - scores)
    logit_grad = jnp.sum(picks * dchosen[:, :, None], axis=1) + 2.0 * ZLOSS * lse * probs
    tokens_full = tokens_in.astype(jnp.float32)
    own_rows = lax.psum_scatter(
        lax.dot_general(tokens_full, logit_grad, (((0,), (0,)), ((), ())), precision=highest),
        "expert",
        scatter_dimension=0,
        tiled=True,
    )
    before = entering(
        own_rows, "dp", lambda earlier, later: earlier + later, jnp.zeros_like(own_rows)
    )
    finished = before + own_rows
    spread = from_root(finished.astype(jnp.bfloat16), "dp", lax.axis_size("dp") - 1).astype(
        finished.dtype
    )
    router_grad = own_columns(spread)
    return (hidden_grad, logit_grad, router_grad)


HINT = {'pack_own': 1073741824,
 'pack': 1073741824,
 'first': 34359738368,
 'join': 1048576,
 'merge': 1024,
 'grads_own': 10737418240,
 'grads_other': 107374182400,
 'prepare': 8589934592,
 'panel': 16777216,
 'hidden': 16777216}
ORDER = (('send', 0), ('first', 0), ('forward', (0,)), ('send', 6), ('send', 1), ('send', 2), ('send', 7),
 ('send', 3), ('forward', (1,)), ('forward', (2,)), ('send', 4), ('send', 5), ('forward', (3,)),
 ('forward', (6,)), ('forward', (7,)), ('forward', (4,)), ('forward', (5,)))
SEND = {7: (('own', 1), ('got', 0)),
 3: (('own', 2),),
 4: (('own', 6), ('other', 0)),
 5: (('own', 7), ('other', 1), ('got', 0), ('saved', 0)),
 2: (('other', 0),)}
FORWARD = {7: (('first', 0),)}
FIRST = (('block', 0),)
SAVED = ()
PARCEL = ()
MERGE = (('own', 5),)


NT = (((1,), (1,)), ((), ()))
NN = (((1,), (0,)), ((), ()))


def kernel_call(body, out_shape, name, flops, touched, *operands, far=(), scratch=(), room=24):
    def space(k, operand):
        if operand.shape == (2,):
            return pltpu.SMEM
        return pltpu.HBM if k in far else pltpu.VMEM

    return pl.pallas_call(
        body,
        out_shape=out_shape,
        in_specs=[pl.BlockSpec(memory_space=space(k, x)) for k, x in enumerate(operands)],
        out_specs=jax.tree.map(lambda _: pl.BlockSpec(memory_space=pltpu.VMEM), out_shape),
        scratch_shapes=scratch,
        compiler_params=pltpu.CompilerParams(vmem_limit_bytes=room * 1024 * 1024),
        cost_estimate=pl.CostEstimate(flops=flops, bytes_accessed=touched, transcendentals=0),
        name=name,
    )(*operands)


def iota(shape, dim):
    return lax.broadcasted_iota(jnp.int32, shape, dim)


def three_halves(value):
    high = value.astype(jnp.bfloat16)
    rest = value - high.astype(jnp.float32)
    middle = rest.astype(jnp.bfloat16)
    low = (rest - middle.astype(jnp.float32)).astype(jnp.bfloat16)
    return high, middle, low


def ranks(chosen):
    tokens = chosen.shape[1]
    before = (iota((tokens, tokens), 0) < iota((tokens, tokens), 1)).astype(jnp.bfloat16)
    return lax.dot_general(
        chosen.astype(jnp.bfloat16), before, NN, preferred_element_type=jnp.float32
    )


def first_body(place_ref, logits_ref, ids_ref, tokens_ref, saved_ref, *outs, flight, cap):
    z_ref, a_ref, gate_ref, saved_own_ref, saved_other_ref, keep_ref, send_ref, turned_ref = outs
    half = saved_own_ref.shape[1]
    for k, out in enumerate((saved_own_ref, saved_other_ref)):
        start = (place_ref[0] if k == 0 else 1 - place_ref[0]) * half
        out[...] = saved_ref[:, pl.ds(pl.multiple_of(start, 128), half)]
    logits = logits_ref[...]
    ids = ids_ref[...]
    experts, tokens = logits.shape
    topk = ids.shape[0]
    top = jnp.max(logits, axis=0, keepdims=True)
    shifted = jnp.exp(logits - top)
    total = jnp.sum(shifted, axis=0, keepdims=True)
    lse = top + jnp.log(total)
    z = (2.0 * ZLOSS) * lse * (shifted / total)
    z_ref[...] = z
    rows = iota((experts, tokens), 0)
    chosen = [
        jnp.sum(jnp.where(rows == ids[k : k + 1], logits, 0.0), axis=0, keepdims=True)
        for k in range(topk)
    ]
    scores = jax.nn.sigmoid(jnp.concatenate(chosen, axis=0))
    ssum = jnp.sum(scores, axis=0, keepdims=True)
    gates = RSCALE * scores / ssum
    slope = (RSCALE / ssum) * scores * (1.0 - scores)
    dense = jnp.zeros((experts, tokens), jnp.float32)
    window = iota((flight, tokens), 0)
    gate_te = jnp.zeros((flight, tokens), jnp.float32)
    picked = jnp.zeros((flight, tokens), jnp.float32)
    for k in range(topk):
        dense = jnp.where(rows == ids[k : k + 1], slope[k : k + 1], dense)
        gate_te = jnp.where(window == ids[k : k + 1], gates[k : k + 1], gate_te)
        picked = jnp.where(window == ids[k : k + 1], 1.0, picked)
    a_ref[...] = dense
    slot = jnp.where(picked > 0.0, ranks(picked), -1.0)
    high, middle, low = three_halves(gate_te)
    lanes = iota((flight, tokens), 1)
    slot_gates = jnp.zeros((flight, tokens), jnp.float32)
    for c in range(cap):
        here = jnp.sum(
            jnp.where(slot == float(c), high.astype(jnp.float32), 0.0), axis=1, keepdims=True
        )
        slot_gates = jnp.where(lanes == c, here, slot_gates)
    gate_ref[...] = slot_gates
    pairs = jnp.concatenate([ids.astype(jnp.float32), slope], axis=0).astype(jnp.bfloat16)
    parts = (z.astype(jnp.bfloat16), pairs, slot.astype(jnp.bfloat16), high, middle, low)
    bundle = jnp.concatenate(parts, axis=0)
    count = 2 * keep_ref.shape[0]
    block = tokens_ref.shape[1] // flight
    turned_ref[...] = tokens_ref[...].T
    for j in range(count):
        parcel = (keep_ref, send_ref)[j % 2]
        there = (place_ref[1] ^ j) & (count - 1)
        for h in range(2):
            start = pl.multiple_of((there + h * count) * block, 32)
            parcel[j // 2, h * block : (h + 1) * block] = turned_ref[pl.ds(start, block)]
        parcel[j // 2, 2 * block : 2 * block + experts + 80] = bundle


def merge_body(keep_ref, got_ref, *outs):
    for q, out in enumerate(outs):
        out[0] = keep_ref[q + 1]
        out[1] = got_ref[q + 1]


def pack_one(me, ids, grad, cap):
    topk, tokens = ids.shape
    wanted = (iota((8, tokens), 0) * 2) ^ me
    picked = jnp.zeros((8, tokens), jnp.float32)
    for k in range(topk):
        picked = jnp.where(wanted == ids[k : k + 1], 1.0, picked)
    slot = jnp.where(picked > 0.0, ranks(picked), -1.0)
    place = iota((cap, tokens), 0).astype(jnp.float32)
    select = jnp.concatenate(
        [jnp.where(slot[q : q + 1] == place, 1.0, 0.0) for q in range(8)], axis=0
    )
    return lax.dot_general(
        select.astype(jnp.bfloat16), grad, NN, preferred_element_type=jnp.float32
    )


def pack_own_body(place_ref, ids_ref, grad_ref, out_ref, *, cap):
    out_ref[...] = pack_one(place_ref[1], ids_ref[...], grad_ref[...], cap)


def pack_body(place_ref, own_ref, ids_ref, grad_ref, *outs, cap):
    peer = pack_one(place_ref[1], ids_ref[...], grad_ref[...], cap)
    for q, out in enumerate(outs):
        rows = slice(q * cap, (q + 1) * cap)
        out[...] = jnp.concatenate([own_ref[rows], peer[rows]], axis=0).astype(jnp.bfloat16)


def swap_matrix(me, size, cap, dtype):
    return (iota((size, size), 1) == (iota((size, size), 0) ^ (me * cap))).astype(dtype)


def finish_grads(me, grads, saved_ref, grads_ref, cap):
    slots = saved_ref.shape[0]
    swap = swap_matrix(me, slots, cap, jnp.bfloat16)
    where_to = swap_matrix(me, slots, cap, jnp.float32)
    saved = lax.dot_general(swap, saved_ref[...], NN, preferred_element_type=jnp.float32)
    grads_ref[...] = grads.astype(grads_ref.dtype)
    sums = jnp.sum(saved * grads, axis=1, keepdims=True)
    return jnp.sum(where_to * sums, axis=0, keepdims=True)


def grads_own_body(place_ref, saved_ref, weight_ref, *refs, cap):
    pieces, (grads_ref, line_ref) = refs[:-2], refs[-2:]
    rows = jnp.concatenate([p[...] for p in pieces], axis=0)
    grads = lax.dot_general(rows, weight_ref[...], NT, preferred_element_type=jnp.float32)
    line_ref[...] = finish_grads(place_ref[1], grads, saved_ref, grads_ref, cap)


def grads_other_body(place_ref, saved_ref, weight_ref, line_own_ref, gate_ref, *refs, cap, spots):
    pieces, (grads_ref, message_ref) = refs[:-2], refs[-2:]
    size = 2 * cap
    rows = jnp.concatenate([pieces[g][k * size : (k + 1) * size] for g, k in spots], axis=0)
    grads = lax.dot_general(rows, weight_ref[...], NT, preferred_element_type=jnp.float32)
    other = finish_grads(place_ref[1], grads, saved_ref, grads_ref, cap)
    own = line_own_ref[...]
    dp = place_ref[0]
    count = message_ref.shape[0] // 2
    for k in range(2):
        line = jnp.where(dp == k, own, other)
        for e in range(count):
            message_ref[k * count + e] = jnp.concatenate([line, gate_ref[e : e + 1]], axis=0)


def hidden_body(place_ref, own_ref, other_ref, message_ref, out_ref, *, cap):
    dp, me = place_ref[0], place_ref[1]
    slots, half = own_ref.shape
    diagonal = iota((cap, slots), 0) == iota((cap, slots), 1)
    columns = []
    for r in range(16):
        line = message_ref[dp * 16 + (me ^ r), 1:2]
        columns.append(jnp.sum(jnp.where(diagonal, line, 0.0), axis=1, keepdims=True))
    gates = jnp.concatenate(columns, axis=0)
    swap = swap_matrix(me, slots, cap, jnp.bfloat16)
    for k, part in enumerate((own_ref, other_ref)):
        value = (gates * part[...].astype(jnp.float32)).astype(jnp.bfloat16)
        value = lax.dot_general(swap, value, NN, preferred_element_type=jnp.float32)
        start = pl.multiple_of((dp if k == 0 else 1 - dp) * half, 128)
        out_ref[:, pl.ds(start, half)] = value.astype(jnp.bfloat16)


def views(parcels):
    return [(parcels[0], 0), (parcels[1], 0)] + [(p, k) for p in parcels[2:] for k in range(2)]


def prepare_body(*refs, experts):
    parcels, (dense_ref, gate_ref) = refs[:5], refs[5:]
    tokens = dense_ref.shape[2]
    at = parcels[0].shape[1] - 80
    rows = iota((experts, tokens), 0).astype(jnp.float32)
    for q, (parcel, here) in enumerate(views(parcels)):
        pairs = parcel[here, at : at + 16].astype(jnp.float32)
        dense = jnp.zeros((experts, tokens), jnp.float32)
        for k in range(8):
            dense = jnp.where(rows == pairs[k : k + 1], pairs[8 + k : 9 + k], dense)
        dense_ref[q] = dense
        gate_ref[q] = sum(
            parcel[here, at + 32 + 16 * k : at + 48 + 16 * k].astype(jnp.float32)
            for k in (2, 1, 0)
        )


def panel_body(place_ref, z_ref, a_ref, message_ref, dense_ref, gate_ref, *refs, cap):
    parcels, logit_ref, outs = refs[:5], refs[5], refs[6:]
    dp, me = place_ref[0], place_ref[1]
    experts, tokens = z_ref.shape
    base = parcels[0].shape[1] - experts - 80
    at = base + experts
    gate_all = jnp.concatenate(
        [message_ref[e, 0:1] + message_ref[16 + e, 0:1] for e in range(16)], axis=0
    )
    swap = swap_matrix(me, gate_all.shape[1], cap, jnp.bfloat16)
    gate_rel = sum(
        lax.dot_general(part, swap, NN, preferred_element_type=jnp.float32)
        for part in three_halves(gate_all)
    )
    lines, blocks = [], []
    total = None
    for q, (parcel, here) in enumerate(views(parcels)):
        slot = parcel[here, at + 16 : at + 32].astype(jnp.float32)
        grad = jnp.zeros((16, tokens), jnp.float32)
        for c in range(cap):
            grad = jnp.where(slot == float(c), gate_rel[:, q * cap + c : q * cap + c + 1], grad)
        mixed = jnp.sum(grad * gate_ref[q], axis=0, keepdims=True) / RSCALE
        spread = jnp.concatenate(
            [grad - mixed, jnp.broadcast_to(-mixed, (experts - 16, tokens))], axis=0
        )
        if q == 0:
            logit_ref[...] = z_ref[...] + a_ref[...] * spread
        line = parcel[here, base:at].astype(jnp.float32) + dense_ref[q] * spread
        lines.append(line.astype(jnp.bfloat16))
        blocks.append(parcel[here, :base])
        if len(lines) == 2:
            part = lax.dot_general(
                jnp.concatenate(lines, axis=1),
                jnp.concatenate(blocks, axis=1),
                NT,
                preferred_element_type=jnp.float32,
            )
            total = part if total is None else total + part
            lines, blocks = [], []
    upper = me >= len(views(parcels))
    columns, width = outs[0].shape
    for k, out in enumerate(outs):
        other_half, other_dp = k // 2, k % 2
        from_upper = upper if other_half == 0 else jnp.logical_not(upper)
        from_second = (dp == 1) if other_dp == 0 else (dp == 0)
        low = jnp.where(from_second, total[columns:, :width], total[:columns, :width])
        high = jnp.where(from_second, total[columns:, width:], total[:columns, width:])
        out[...] = jnp.where(from_upper, high, low).astype(out.dtype)


def join_body(*refs):
    refs[-1][...] = jnp.concatenate([ref[...] for ref in refs[:-1]], axis=0)


def over_dp(value):
    return lax.ppermute(value, "dp", [(0, 1), (1, 0)])


def over_expert(value, bits):
    count = lax.axis_size("expert")
    return lax.ppermute(value, "expert", [(k, k ^ bits) for k in range(count)])


def over_both(value, dp_bit, bits):
    count = lax.axis_size("expert")
    return lax.ppermute(
        value, ("dp", "expert"), [(k, k ^ (dp_bit * count + bits)) for k in range(2 * count)]
    )


def after(value, *earlier):
    return lax.optimization_barrier((value, *earlier))[0]


def paired_local(tokens_in, out_grad, router_logits, expert_ids, saved_hidden, down_weight):
    flight = lax.axis_size("expert")
    cap, hidden = saved_hidden.shape[3:]
    tokens, width = out_grad.shape
    experts = router_logits.shape[1]
    half, group = hidden // 2, flight // 2
    slots = flight * cap
    block = width // flight
    f32, bf16 = jnp.float32, jnp.bfloat16
    dp, me = lax.axis_index("dp"), lax.axis_index("expert")
    place = jnp.stack([dp, me]).astype(jnp.int32)
    weight = down_weight[0]
    logits_t, ids_t = router_logits.T, expert_ids.T
    saved = saved_hidden.reshape(slots, hidden)

    grad_peer = over_expert(out_grad, 1)
    ids_peer = over_expert(ids_t, 1)
    packed = kernel_call(
        lambda *refs: pack_own_body(*refs, cap=cap),
        jax.ShapeDtypeStruct((slots // 2, width), f32),
        "pack_own", HINT["pack_own"], 3 << 20, place, ids_t, out_grad,
    )
    blocks = kernel_call(
        lambda *refs: pack_body(*refs, cap=cap),
        tuple(jax.ShapeDtypeStruct((2 * cap, width), bf16) for _ in range(8)),
        "pack", HINT["pack"], 3 << 20, place, packed, ids_peer, grad_peer,
    )
    known = {("block", 0): blocks[0]}

    def parcel_shape(count):
        return jax.ShapeDtypeStruct((count, 2 * block + experts + 80, tokens), bf16)

    def held(value, waits):
        return after(value, *(known[w] for w in waits)) if waits else value

    def send(q):
        known["own", q] = over_expert(held(blocks[q], SEND.get(q, ())), 2 * q) if q else blocks[0]

    def forward(group):
        pieces = [known["own", q] for q in group]
        if len(pieces) > 1:
            pieces = [
                kernel_call(
                    join_body,
                    jax.ShapeDtypeStruct((2 * cap * len(pieces), width), bf16),
                    "join", HINT["join"], 1 << 20, *pieces,
                )
            ]
        known["other", group[0]] = over_dp(held(pieces[0], FORWARD.get(group[0], ())))

    def first():
        nonlocal logits_t, tokens_in, saved
        logits_t, tokens_in, saved = held((logits_t, tokens_in, saved), FIRST)
        outs = kernel_call(
            lambda *refs: first_body(*refs, flight=flight, cap=cap),
            (
                jax.ShapeDtypeStruct((experts, tokens), f32),
                jax.ShapeDtypeStruct((experts, tokens), f32),
                jax.ShapeDtypeStruct((flight, tokens), f32),
                jax.ShapeDtypeStruct((slots, half), bf16),
                jax.ShapeDtypeStruct((slots, half), bf16),
                *(parcel_shape(group // 2),) * 2,
            ),
            "first", HINT["first"], 3 << 20, place, logits_t, ids_t, tokens_in, saved,
            scratch=[pltpu.VMEM((width, tokens), bf16)],
        )
        known["first", 0] = outs[2]
        known["results", 0] = outs
        known["saved", 0] = over_dp(held(outs[4], SAVED))
        known["got", 0] = over_expert(held(outs[6], PARCEL), 1)

    for kind, which in ORDER:
        {"send": send, "forward": forward, "first": lambda _: first()}[kind](which)
    z, a, slot_gates, saved_own, _, parcel_keep, _ = known["results", 0]
    own = [known["own", q] for q in range(8)]
    groups = [which for kind, which in ORDER if kind == "forward"]
    other = [known["other", members[0]] for members in groups]
    found = {q: (g, k) for g, members in enumerate(groups) for k, q in enumerate(members)}
    spots = [found[q] for q in range(8)]
    saved_other, parcel_got = known["saved", 0], known["got", 0]
    merged = kernel_call(
        merge_body, (parcel_shape(2),) * 3, "merge", HINT["merge"], 4 << 20,
        held(parcel_keep, MERGE), parcel_got,
    )
    parcels = (parcel_keep, parcel_got, *(over_expert(m, 2 * q + 2) for q, m in enumerate(merged)))
    grads_own, line_own = kernel_call(
        lambda *refs: grads_own_body(*refs, cap=cap),
        (jax.ShapeDtypeStruct((slots, half), f32), jax.ShapeDtypeStruct((1, slots), f32)),
        "grads_own", HINT["grads_own"], 5 << 20, place, saved_own, weight, *own,
    )
    grads_other, message = kernel_call(
        lambda *refs: grads_other_body(*refs, cap=cap, spots=spots),
        (
            jax.ShapeDtypeStruct((slots, half), bf16),
            jax.ShapeDtypeStruct((2 * flight, 2, slots), f32),
        ),
        "grads_other", HINT["grads_other"], 5 << 20,
        place, saved_other, weight, line_own, slot_gates, *other,
    )
    grads_back = over_dp(grads_other)
    message = lax.all_to_all(message, ("dp", "expert"), 0, 0, tiled=True)
    message, grads_back = lax.optimization_barrier((message, grads_back))
    dense, gates = kernel_call(
        lambda *refs: prepare_body(*refs, experts=experts),
        (
            jax.ShapeDtypeStruct((group, experts, tokens), f32),
            jax.ShapeDtypeStruct((group, 16, tokens), f32),
        ),
        "prepare", HINT["prepare"], 1 << 20, *parcels,
    )
    logit_t, *sums = kernel_call(
        lambda *refs: panel_body(*refs, cap=cap),
        (
            jax.ShapeDtypeStruct((experts, tokens), f32),
            jax.ShapeDtypeStruct((experts // 2, block), f32),
            *(jax.ShapeDtypeStruct((experts // 2, block), bf16) for _ in range(3)),
        ),
        "panel", HINT["panel"], 4 << 20,
        place, z, a, message, dense, gates, *parcels,
    )
    hidden_grad = kernel_call(
        lambda *refs: hidden_body(*refs, cap=cap),
        jax.ShapeDtypeStruct((slots, hidden), bf16),
        "hidden", HINT["hidden"], 1 << 20,
        place, grads_own, grads_back, message,
    )
    far = [over_both(sums[3], 1, group), over_both(sums[2], 0, group), over_both(sums[1], 1, 0)]
    router_t = after(sums[0], hidden_grad) + sum(part.astype(f32) for part in far)
    return (
        hidden_grad.reshape(1, 1, flight, cap, hidden),
        logit_t.T,
        router_t.T,
    )


def solution(mesh):
    in_specs = (
        P(("dp", "expert"), None),
        P(("dp", "expert"), None),
        P(("dp", "expert"), None),
        P(("dp", "expert"), None),
        P("dp", "expert", None, None, None),
        P("expert", "dp", None),
    )
    out_specs = (P("dp", "expert", None, None, None), P(("dp", "expert"), None), P("expert", "dp"))
    paired = mesh.shape["dp"] == 2 and mesh.shape["expert"] == 16
    local = paired_local if paired else general_local
    return jax.shard_map(local, mesh=mesh, in_specs=in_specs, out_specs=out_specs, check_vma=False)
```

```python
import jax
import jax.numpy as jnp
from jax import lax
from jax.experimental import pallas as pl
from jax.experimental.pallas import tpu as pltpu
from jax.sharding import PartitionSpec as P

RSCALE = 2.827
ZLOSS = 0.25


def entering(shard, axis, combine, identity):
    length, place = (lax.axis_size(axis), lax.axis_index(axis))
    everything = lax.all_gather(shard.astype(jnp.bfloat16), axis)
    start = jnp.broadcast_to(jnp.asarray(identity, shard.dtype), shard.shape)

    def lap(k, before):
        reached = k < place
        new = combine(before, everything[k].astype(shard.dtype))
        return jnp.where(reached, new, before)

    return lax.fori_loop(0, length, lap, start)


def from_root(value, axis, source):
    kept = jnp.where(lax.axis_index(axis) == source, value, 0).astype(value.dtype)
    return lax.psum(kept, axis)


def slot_table(ids_block, flight, cap):
    owners = jnp.arange(flight, dtype=jnp.int32)
    chosen = jnp.any(ids_block[:, :, None] == owners[None, None, :], axis=1)
    as_int = chosen.astype(jnp.int32)
    rank = jnp.cumsum(as_int, axis=0) - as_int
    places = jnp.arange(cap, dtype=jnp.int32)
    table = chosen[None, :, :] & (rank[None, :, :] == places[:, None, None])
    return jnp.transpose(table, (2, 0, 1))


def own_columns(panel):
    count = panel.shape[1] // lax.axis_size("dp")
    return lax.dynamic_slice_in_dim(panel, lax.axis_index("dp") * count, count, 1)


def general_local(tokens_in, out_grad, router_logits, expert_ids, saved_hidden, down_weight):
    highest = lax.Precision.HIGHEST
    flight = lax.axis_size("expert")
    cap = saved_hidden.shape[3]
    hidden = saved_hidden.shape[4]
    width = out_grad.shape[1]
    experts = router_logits.shape[1]
    top = jnp.max(router_logits, axis=1, keepdims=True)
    shifted = jnp.exp(router_logits - top)
    total = jnp.sum(shifted, axis=1, keepdims=True)
    probs = shifted / total
    lse = top + jnp.log(total)
    columns = jnp.arange(experts, dtype=jnp.int32)
    picks = (expert_ids[:, :, None] == columns[None, None, :]).astype(jnp.float32)
    chosen_logit = jnp.sum(picks * router_logits[:, None, :], axis=2)
    scores = jax.nn.sigmoid(chosen_logit)
    ssum = jnp.sum(scores, axis=1, keepdims=True)
    gates = RSCALE * scores / ssum
    gate_half = gates.astype(jnp.bfloat16)
    in_window = picks[:, :, :flight]
    gate_te = jnp.sum(in_window * gate_half.astype(jnp.float32)[:, :, None], axis=1)
    table = slot_table(expert_ids, flight, cap)
    table_half = table.astype(jnp.bfloat16)
    table_full = table.astype(jnp.float32)
    send_rows = jnp.einsum(
        "ect,td->ecd", table_half, out_grad, preferred_element_type=jnp.float32
    ).astype(jnp.bfloat16)
    send_gates = jnp.einsum("ect,te->ec", table_full, gate_te, precision=highest).astype(
        jnp.bfloat16
    )
    recv_rows, recv_gates = (
        lax.all_to_all(send_rows, "expert", split_axis=0, concat_axis=0, tiled=True),
        lax.all_to_all(send_gates, "expert", split_axis=0, concat_axis=0, tiled=True),
    )
    flat_rows = recv_rows.reshape(flight * cap, width)
    part = lax.dot_general(
        flat_rows,
        lax.all_gather(down_weight, "dp", axis=1, tiled=True)[0],
        (((1,), (1,)), ((), ())),
        preferred_element_type=jnp.float32,
    )
    slot_gates = recv_gates.reshape(flight * cap, 1).astype(jnp.float32)
    hidden_grad = (slot_gates * part).astype(jnp.bfloat16).reshape(1, 1, flight, cap, hidden)
    saved_flat = saved_hidden.reshape(flight * cap, hidden)
    gate_grad = jnp.sum(saved_flat * part, axis=1).reshape(flight, cap)
    returned = lax.all_to_all(gate_grad, "expert", split_axis=0, concat_axis=0, tiled=True)
    grad_te = jnp.einsum("ect,ec->te", table_full, returned, precision=highest)
    grad_choice = jnp.sum(in_window * grad_te[:, None, :], axis=2)
    mixed = jnp.sum(grad_choice * gates, axis=1, keepdims=True) / RSCALE
    dscore = RSCALE / ssum * (grad_choice - mixed)
    dchosen = dscore * scores * (1.0 - scores)
    logit_grad = jnp.sum(picks * dchosen[:, :, None], axis=1) + 2.0 * ZLOSS * lse * probs
    tokens_full = tokens_in.astype(jnp.float32)
    own_rows = lax.psum_scatter(
        lax.dot_general(tokens_full, logit_grad, (((0,), (0,)), ((), ())), precision=highest),
        "expert",
        scatter_dimension=0,
        tiled=True,
    )
    before = entering(
        own_rows, "dp", lambda earlier, later: earlier + later, jnp.zeros_like(own_rows)
    )
    finished = before + own_rows
    spread = from_root(finished.astype(jnp.bfloat16), "dp", lax.axis_size("dp") - 1).astype(
        finished.dtype
    )
    router_grad = own_columns(spread)
    return (hidden_grad, logit_grad, router_grad)


HINT = {'pack_own': 1073741824,
 'pack': 1073741824,
 'first': 34359738368,
 'join': 1048576,
 'merge': 1024,
 'grads_own': 10737418240,
 'grads_other': 107374182400,
 'prepare': 8589934592,
 'panel': 1073741824,
 'hidden': 16777216}
ORDER = (('send', 0), ('first', 0), ('forward', (0,)), ('send', 6), ('send', 1), ('send', 2), ('send', 7),
 ('send', 3), ('forward', (1,)), ('forward', (2,)), ('send', 4), ('send', 5), ('forward', (3,)),
 ('forward', (6,)), ('forward', (7,)), ('forward', (4,)), ('forward', (5,)))
SEND = {7: (('own', 1), ('got', 0)),
 3: (('own', 2),),
 4: (('own', 6), ('other', 0)),
 5: (('own', 7), ('other', 1), ('got', 0), ('saved', 0)),
 2: (('other', 0),)}
FORWARD = {7: (('first', 0),)}
FIRST = (('block', 0),)
MERGE = (('own', 5),)
STEPS = 7


NT = (((1,), (1,)), ((), ()))
NN = (((1,), (0,)), ((), ()))


def kernel_call(body, out_shape, name, flops, touched, *operands, far=(), scratch=(), room=24):
    def space(k, operand):
        if operand.shape == (2,):
            return pltpu.SMEM
        return pltpu.HBM if k in far else pltpu.VMEM

    return pl.pallas_call(
        body,
        out_shape=out_shape,
        in_specs=[pl.BlockSpec(memory_space=space(k, x)) for k, x in enumerate(operands)],
        out_specs=jax.tree.map(lambda _: pl.BlockSpec(memory_space=pltpu.VMEM), out_shape),
        scratch_shapes=scratch,
        compiler_params=pltpu.CompilerParams(vmem_limit_bytes=room * 1024 * 1024),
        cost_estimate=pl.CostEstimate(flops=flops, bytes_accessed=touched, transcendentals=0),
        name=name,
    )(*operands)


def iota(shape, dim):
    return lax.broadcasted_iota(jnp.int32, shape, dim)


def three_halves(value):
    high = value.astype(jnp.bfloat16)
    rest = value - high.astype(jnp.float32)
    middle = rest.astype(jnp.bfloat16)
    low = (rest - middle.astype(jnp.float32)).astype(jnp.bfloat16)
    return high, middle, low


def ranks(chosen):
    tokens = chosen.shape[1]
    before = (iota((tokens, tokens), 0) < iota((tokens, tokens), 1)).astype(jnp.bfloat16)
    return lax.dot_general(
        chosen.astype(jnp.bfloat16), before, NN, preferred_element_type=jnp.float32
    )


def first_body(place_ref, logits_ref, ids_ref, tokens_ref, saved_ref, *outs, flight, cap):
    z_ref, a_ref, gate_ref, saved_own_ref, saved_other_ref, keep_ref, send_ref, turned_ref = outs
    half = saved_own_ref.shape[1]
    for k, out in enumerate((saved_own_ref, saved_other_ref)):
        start = (place_ref[0] if k == 0 else 1 - place_ref[0]) * half
        out[...] = saved_ref[:, pl.ds(pl.multiple_of(start, 128), half)]
    logits = logits_ref[...]
    ids = ids_ref[...]
    experts, tokens = logits.shape
    topk = ids.shape[0]
    top = jnp.max(logits, axis=0, keepdims=True)
    shifted = jnp.exp(logits - top)
    total = jnp.sum(shifted, axis=0, keepdims=True)
    lse = top + jnp.log(total)
    z = (2.0 * ZLOSS) * lse * (shifted / total)
    z_ref[...] = z
    rows = iota((experts, tokens), 0)
    chosen = [
        jnp.sum(jnp.where(rows == ids[k : k + 1], logits, 0.0), axis=0, keepdims=True)
        for k in range(topk)
    ]
    scores = jax.nn.sigmoid(jnp.concatenate(chosen, axis=0))
    ssum = jnp.sum(scores, axis=0, keepdims=True)
    gates = RSCALE * scores / ssum
    slope = (RSCALE / ssum) * scores * (1.0 - scores)
    dense = jnp.zeros((experts, tokens), jnp.float32)
    window = iota((flight, tokens), 0)
    gate_te = jnp.zeros((flight, tokens), jnp.float32)
    picked = jnp.zeros((flight, tokens), jnp.float32)
    for k in range(topk):
        dense = jnp.where(rows == ids[k : k + 1], slope[k : k + 1], dense)
        gate_te = jnp.where(window == ids[k : k + 1], gates[k : k + 1], gate_te)
        picked = jnp.where(window == ids[k : k + 1], 1.0, picked)
    a_ref[...] = dense
    slot = jnp.where(picked > 0.0, ranks(picked), -1.0)
    high, middle, low = three_halves(gate_te)
    lanes = iota((flight, tokens), 1)
    slot_gates = jnp.zeros((flight, tokens), jnp.float32)
    for c in range(cap):
        here = jnp.sum(
            jnp.where(slot == float(c), high.astype(jnp.float32), 0.0), axis=1, keepdims=True
        )
        slot_gates = jnp.where(lanes == c, here, slot_gates)
    gate_ref[...] = slot_gates
    pairs = jnp.concatenate([ids.astype(jnp.float32), slope], axis=0).astype(jnp.bfloat16)
    parts = (z.astype(jnp.bfloat16), pairs, slot.astype(jnp.bfloat16), high, middle, low)
    bundle = jnp.concatenate(parts, axis=0)
    count = 2 * keep_ref.shape[0]
    block = tokens_ref.shape[1] // flight
    turned_ref[...] = tokens_ref[...].T
    for j in range(count):
        parcel = (keep_ref, send_ref)[j % 2]
        there = (place_ref[1] ^ j) & (count - 1)
        for h in range(2):
            start = pl.multiple_of((there + h * count) * block, 32)
            parcel[j // 2, h * block : (h + 1) * block] = turned_ref[pl.ds(start, block)]
        parcel[j // 2, 2 * block : 2 * block + experts + 80] = bundle


def merge_body(keep_ref, got_ref, *outs):
    for q, out in enumerate(outs):
        out[0] = keep_ref[q + 1]
        out[1] = got_ref[q + 1]


def pack_one(me, ids, grad, cap):
    topk, tokens = ids.shape
    wanted = (iota((8, tokens), 0) * 2) ^ me
    picked = jnp.zeros((8, tokens), jnp.float32)
    for k in range(topk):
        picked = jnp.where(wanted == ids[k : k + 1], 1.0, picked)
    slot = jnp.where(picked > 0.0, ranks(picked), -1.0)
    place = iota((cap, tokens), 0).astype(jnp.float32)
    select = jnp.concatenate(
        [jnp.where(slot[q : q + 1] == place, 1.0, 0.0) for q in range(8)], axis=0
    )
    return lax.dot_general(
        select.astype(jnp.bfloat16), grad, NN, preferred_element_type=jnp.float32
    )


def pack_own_body(place_ref, ids_ref, grad_ref, out_ref, *, cap):
    out_ref[...] = pack_one(place_ref[1], ids_ref[...], grad_ref[...], cap)


def pack_body(place_ref, own_ref, ids_ref, grad_ref, *outs, cap):
    peer = pack_one(place_ref[1], ids_ref[...], grad_ref[...], cap)
    for q, out in enumerate(outs):
        rows = slice(q * cap, (q + 1) * cap)
        out[...] = jnp.concatenate([own_ref[rows], peer[rows]], axis=0).astype(jnp.bfloat16)


def swap_matrix(me, size, cap, dtype):
    return (iota((size, size), 1) == (iota((size, size), 0) ^ (me * cap))).astype(dtype)


def multiply(pieces, weight_ref, steps):
    width = weight_ref.shape[1] // steps
    total = None
    for k in range(steps):
        part = slice(k * width, (k + 1) * width)
        rows = jnp.concatenate([p[:, part] for p in pieces], axis=0)
        term = lax.dot_general(rows, weight_ref[:, part], NT, preferred_element_type=jnp.float32)
        total = term if total is None else total + term
    return total


def slot_line(me, saved, grads, cap):
    sums = jnp.sum(saved * grads, axis=1, keepdims=True)
    where_to = swap_matrix(me, grads.shape[0], cap, jnp.float32)
    return jnp.sum(where_to * sums, axis=0, keepdims=True)


def grads_own_body(place_ref, saved_ref, saved_other_ref, weight_ref, *refs, cap, steps):
    pieces, (grads_ref, line_ref, turned_ref) = refs[:-3], refs[-3:]
    grads = multiply(pieces, weight_ref, steps)
    swap = swap_matrix(place_ref[1], grads.shape[0], cap, jnp.bfloat16)
    saved, turned = (
        lax.dot_general(swap, ref[...], NN, preferred_element_type=jnp.float32)
        for ref in (saved_ref, saved_other_ref)
    )
    turned_ref[...] = turned
    grads_ref[...] = grads
    line_ref[...] = slot_line(place_ref[1], saved, grads, cap)


def grads_other_body(place_ref, turned_ref, weight_ref, line_own_ref, gate_ref, *refs, cap, spots, steps):
    groups, (grads_ref, message_ref) = refs[:-2], refs[-2:]
    size = 2 * cap
    pieces = [groups[g].at[k * size : (k + 1) * size] for g, k in spots]
    grads = multiply(pieces, weight_ref, steps)
    grads_ref[...] = grads.astype(grads_ref.dtype)
    other = slot_line(place_ref[1], turned_ref[...], grads, cap)
    own = line_own_ref[...]
    dp = place_ref[0]
    count = message_ref.shape[0] // 2
    for k in range(2):
        line = jnp.where(dp == k, own, other)
        for e in range(count):
            message_ref[k * count + e] = jnp.concatenate([line, gate_ref[e : e + 1]], axis=0)


def hidden_body(place_ref, own_ref, other_ref, message_ref, out_ref, *, cap):
    dp, me = place_ref[0], place_ref[1]
    slots, half = own_ref.shape
    diagonal = iota((cap, slots), 0) == iota((cap, slots), 1)
    columns = []
    for r in range(16):
        line = message_ref[dp * 16 + (me ^ r), 1:2]
        columns.append(jnp.sum(jnp.where(diagonal, line, 0.0), axis=1, keepdims=True))
    gates = jnp.concatenate(columns, axis=0)
    swap = swap_matrix(me, slots, cap, jnp.bfloat16)
    for k, part in enumerate((own_ref, other_ref)):
        value = (gates * part[...].astype(jnp.float32)).astype(jnp.bfloat16)
        value = lax.dot_general(swap, value, NN, preferred_element_type=jnp.float32)
        start = pl.multiple_of((dp if k == 0 else 1 - dp) * half, 128)
        out_ref[:, pl.ds(start, half)] = value.astype(jnp.bfloat16)


def views(parcels):
    return [(parcels[0], 0), (parcels[1], 0)] + [(p, k) for p in parcels[2:] for k in range(2)]


def prepare_body(*refs, experts):
    parcels, (dense_ref, gate_ref) = refs[:5], refs[5:]
    tokens = dense_ref.shape[2]
    at = parcels[0].shape[1] - 80
    rows = iota((experts, tokens), 0).astype(jnp.float32)
    for q, (parcel, here) in enumerate(views(parcels)):
        pairs = parcel[here, at : at + 16].astype(jnp.float32)
        dense = jnp.zeros((experts, tokens), jnp.float32)
        for k in range(8):
            dense = jnp.where(rows == pairs[k : k + 1], pairs[8 + k : 9 + k], dense)
        dense_ref[q] = dense
        gate_ref[q] = sum(
            parcel[here, at + 32 + 16 * k : at + 48 + 16 * k].astype(jnp.float32)
            for k in (2, 1, 0)
        )


def panel_body(place_ref, z_ref, a_ref, message_ref, dense_ref, gate_ref, *refs, cap):
    parcels, logit_ref, outs = refs[:5], refs[5], refs[6:]
    dp, me = place_ref[0], place_ref[1]
    experts, tokens = z_ref.shape
    base = parcels[0].shape[1] - experts - 80
    at = base + experts
    gate_all = jnp.concatenate(
        [message_ref[e, 0:1] + message_ref[16 + e, 0:1] for e in range(16)], axis=0
    )
    gate_rel = gate_all
    lanes = iota(gate_all.shape, 1)
    size = gate_all.shape[1]
    for bit in range(4):
        step = cap << bit
        swapped = jnp.where(
            (lanes & step) != 0,
            pltpu.roll(gate_rel, step, 1),
            pltpu.roll(gate_rel, size - step, 1),
        )
        gate_rel = jnp.where(((me >> bit) & 1) == 1, swapped, gate_rel)
    lines, blocks = [], []
    total = None
    for q, (parcel, here) in enumerate(views(parcels)):
        slot = parcel[here, at + 16 : at + 32].astype(jnp.float32)
        grad = jnp.zeros((16, tokens), jnp.float32)
        for c in range(cap):
            grad = jnp.where(slot == float(c), gate_rel[:, q * cap + c : q * cap + c + 1], grad)
        mixed = jnp.sum(grad * gate_ref[q], axis=0, keepdims=True) / RSCALE
        spread = jnp.concatenate(
            [grad - mixed, jnp.broadcast_to(-mixed, (experts - 16, tokens))], axis=0
        )
        if q == 0:
            logit_ref[...] = z_ref[...] + a_ref[...] * spread
        line = parcel[here, base:at].astype(jnp.float32) + dense_ref[q] * spread
        lines.append(line.astype(jnp.bfloat16))
        blocks.append(parcel[here, :base])
        if len(lines) == 2:
            part = lax.dot_general(
                jnp.concatenate(lines, axis=1),
                jnp.concatenate(blocks, axis=1),
                NT,
                preferred_element_type=jnp.float32,
            )
            total = part if total is None else total + part
            lines, blocks = [], []
    upper = me >= len(views(parcels))
    columns, width = outs[0].shape
    for k, out in enumerate(outs):
        other_half, other_dp = k // 2, k % 2
        from_upper = upper if other_half == 0 else jnp.logical_not(upper)
        from_second = (dp == 1) if other_dp == 0 else (dp == 0)
        low = jnp.where(from_second, total[columns:, :width], total[:columns, :width])
        high = jnp.where(from_second, total[columns:, width:], total[:columns, width:])
        out[...] = jnp.where(from_upper, high, low).astype(out.dtype)


def join_body(*refs):
    refs[-1][...] = jnp.concatenate([ref[...] for ref in refs[:-1]], axis=0)


def over_dp(value):
    return lax.ppermute(value, "dp", [(0, 1), (1, 0)])


def over_expert(value, bits):
    count = lax.axis_size("expert")
    return lax.ppermute(value, "expert", [(k, k ^ bits) for k in range(count)])


def over_both(value, dp_bit, bits):
    count = lax.axis_size("expert")
    return lax.ppermute(
        value, ("dp", "expert"), [(k, k ^ (dp_bit * count + bits)) for k in range(2 * count)]
    )


def after(value, *earlier):
    return lax.optimization_barrier((value, *earlier))[0]


def paired_local(tokens_in, out_grad, router_logits, expert_ids, saved_hidden, down_weight):
    flight = lax.axis_size("expert")
    cap, hidden = saved_hidden.shape[3:]
    tokens, width = out_grad.shape
    experts = router_logits.shape[1]
    half, group = hidden // 2, flight // 2
    slots = flight * cap
    block = width // flight
    f32, bf16 = jnp.float32, jnp.bfloat16
    dp, me = lax.axis_index("dp"), lax.axis_index("expert")
    place = jnp.stack([dp, me]).astype(jnp.int32)
    weight = down_weight[0]
    logits_t, ids_t = router_logits.T, expert_ids.T
    saved = saved_hidden.reshape(slots, hidden)

    grad_peer = over_expert(out_grad, 1)
    ids_peer = over_expert(ids_t, 1)
    packed = kernel_call(
        lambda *refs: pack_own_body(*refs, cap=cap),
        jax.ShapeDtypeStruct((slots // 2, width), f32),
        "pack_own", HINT["pack_own"], 3 << 20, place, ids_t, out_grad,
    )
    blocks = kernel_call(
        lambda *refs: pack_body(*refs, cap=cap),
        tuple(jax.ShapeDtypeStruct((2 * cap, width), bf16) for _ in range(8)),
        "pack", HINT["pack"], 3 << 20, place, packed, ids_peer, grad_peer,
    )
    known = {("block", 0): blocks[0]}

    def parcel_shape(count):
        return jax.ShapeDtypeStruct((count, 2 * block + experts + 80, tokens), bf16)

    def held(value, waits):
        return after(value, *(known[w] for w in waits)) if waits else value

    def send(q):
        known["own", q] = over_expert(held(blocks[q], SEND.get(q, ())), 2 * q) if q else blocks[0]

    def forward(group):
        pieces = [known["own", q] for q in group]
        if len(pieces) > 1:
            pieces = [
                kernel_call(
                    join_body,
                    jax.ShapeDtypeStruct((2 * cap * len(pieces), width), bf16),
                    "join", HINT["join"], 1 << 20, *pieces,
                )
            ]
        known["other", group[0]] = over_dp(held(pieces[0], FORWARD.get(group[0], ())))

    def first():
        nonlocal logits_t, tokens_in, saved
        logits_t, tokens_in, saved = held((logits_t, tokens_in, saved), FIRST)
        outs = kernel_call(
            lambda *refs: first_body(*refs, flight=flight, cap=cap),
            (
                jax.ShapeDtypeStruct((experts, tokens), f32),
                jax.ShapeDtypeStruct((experts, tokens), f32),
                jax.ShapeDtypeStruct((flight, tokens), f32),
                jax.ShapeDtypeStruct((slots, half), bf16),
                jax.ShapeDtypeStruct((slots, half), bf16),
                *(parcel_shape(group // 2),) * 2,
            ),
            "first", HINT["first"], 3 << 20, place, logits_t, ids_t, tokens_in, saved,
            scratch=[pltpu.VMEM((width, tokens), bf16)],
        )
        known["first", 0] = outs[2]
        known["results", 0] = outs
        known["saved", 0] = over_dp(outs[4])
        known["got", 0] = over_expert(outs[6], 1)

    for kind, which in ORDER:
        {"send": send, "forward": forward, "first": lambda _: first()}[kind](which)
    z, a, slot_gates, saved_own, _, parcel_keep, _ = known["results", 0]
    own = [known["own", q] for q in range(8)]
    groups = [which for kind, which in ORDER if kind == "forward"]
    other = [known["other", members[0]] for members in groups]
    found = {q: (g, k) for g, members in enumerate(groups) for k, q in enumerate(members)}
    spots = [found[q] for q in range(8)]
    saved_other, parcel_got = known["saved", 0], known["got", 0]
    merged = kernel_call(
        merge_body, (parcel_shape(2),) * 3, "merge", HINT["merge"], 4 << 20,
        held(parcel_keep, MERGE), parcel_got,
    )
    parcels = (parcel_keep, parcel_got, *(over_expert(m, 2 * q + 2) for q, m in enumerate(merged)))
    grads_own, line_own, saved_turned = kernel_call(
        lambda *refs: grads_own_body(*refs, cap=cap, steps=STEPS),
        (
            jax.ShapeDtypeStruct((slots, half), f32),
            jax.ShapeDtypeStruct((1, slots), f32),
            jax.ShapeDtypeStruct((slots, half), f32),
        ),
        "grads_own", HINT["grads_own"], 5 << 20, place, saved_own, saved_other, weight, *own,
    )
    grads_other, message = kernel_call(
        lambda *refs: grads_other_body(*refs, cap=cap, spots=spots, steps=STEPS),
        (
            jax.ShapeDtypeStruct((slots, half), bf16),
            jax.ShapeDtypeStruct((2 * flight, 2, slots), f32),
        ),
        "grads_other", HINT["grads_other"], 5 << 20,
        place, saved_turned, weight, line_own, slot_gates, *other,
    )
    grads_back = over_dp(grads_other)
    message = lax.all_to_all(message, ("dp", "expert"), 0, 0, tiled=True)
    message, grads_back = lax.optimization_barrier((message, grads_back))
    dense, gates = kernel_call(
        lambda *refs: prepare_body(*refs, experts=experts),
        (
            jax.ShapeDtypeStruct((group, experts, tokens), f32),
            jax.ShapeDtypeStruct((group, 16, tokens), f32),
        ),
        "prepare", HINT["prepare"], 1 << 20, *parcels,
    )
    logit_t, *sums = kernel_call(
        lambda *refs: panel_body(*refs, cap=cap),
        (
            jax.ShapeDtypeStruct((experts, tokens), f32),
            jax.ShapeDtypeStruct((experts // 2, block), f32),
            *(jax.ShapeDtypeStruct((experts // 2, block), bf16) for _ in range(3)),
        ),
        "panel", HINT["panel"], 4 << 20,
        place, z, a, message, dense, gates, *parcels,
    )
    hidden_grad = kernel_call(
        lambda *refs: hidden_body(*refs, cap=cap),
        jax.ShapeDtypeStruct((slots, hidden), bf16),
        "hidden", HINT["hidden"], 1 << 20,
        place, grads_own, grads_back, message,
    )
    moves = {1: (1, 0), 2: (0, group), 3: (1, group)}
    far = [over_both(sums[k], *moves[k]) for k in (3, 1, 2)]
    router_t = after(sums[0], hidden_grad) + sum(part.astype(f32) for part in far)
    return (
        hidden_grad.reshape(1, 1, flight, cap, hidden),
        logit_t.T,
        router_t.T,
    )


def solution(mesh):
    in_specs = (
        P(("dp", "expert"), None),
        P(("dp", "expert"), None),
        P(("dp", "expert"), None),
        P(("dp", "expert"), None),
        P("dp", "expert", None, None, None),
        P("expert", "dp", None),
    )
    out_specs = (P("dp", "expert", None, None, None), P(("dp", "expert"), None), P("expert", "dp"))
    paired = mesh.shape["dp"] == 2 and mesh.shape["expert"] == 16
    local = paired_local if paired else general_local
    return jax.shard_map(local, mesh=mesh, in_specs=in_specs, out_specs=out_specs, check_vma=False)
```
